128 devices in a mesh: users: 32 (over z, x, core), items: 4 (over y).
Axes of the slice: x: 4, y: 4, z: 4, core: 2. Of those that a mesh axis runs over, the one named last changes fastest.
Arguments:
- user_old: float32 [32768, 128], P(('users', 'items')), may hold values from -3 to 3
- item_old: float32 [65536, 128], P(('users', 'items'))
- item_rhs: float32 [65536, 128], P(('users', 'items')), may hold values from -360 to 360
- user_gram: float32 [128, 128], replicated
- req_count: int32 [128, 128], P(('users', 'items')), may hold values from 1 to 16, as said below
- req_item: int32 [128, 128, 16], P(('users', 'items')), may hold values from 0 to 511
- req_user: int32 [128, 128, 16], P(('users', 'items')), may hold values from 0 to 255
- weight: float32 [128, 128, 16], P(('users', 'items')), may hold values from 1 to 20
- rating: float32 [128, 128, 16], P(('users', 'items')), may hold values from -4 to 4
Outputs:
- user_new: float32 [32768, 128], P(('users', 'items'))
- item_new: float32 [65536, 128], P(('users', 'items'))
The draws below stay inside these ranges and needn't reach their ends.
Inputs may be any that keep to these rules, and one draw needn't show every extreme that they name: In every draw some item owner receives 16 live slots from every device; every other count lies between 1 and 16. Only the first req_count[d, o] slots of a pair carry a rating.
All inputs are finite; a program needn't handle non-finite values.
Results may differ from the reference program's by a relative error of at most 0.0003.
Values sent between devices are 32-bit elements; how exact they have to be, the bound alone decides.
A program may use at most 64 MiB of HBM per device.

```python
import math
import jax
import jax.numpy as jnp
from jax import lax

R = 128
ITERS = 8
U_DEV = 256
ITEM_DEV = 512
NDEV = 128
CAP = 16
USERS = 32768
ITEMS = 65536


def draw_item_old(key, part):
    key_col, key_val = jax.random.split(jax.random.fold_in(key, 11))
    column_scale = jnp.exp(jax.random.uniform(key_col, (R,), jnp.float32, math.log(0.3), 0.0))
    position = jnp.arange(ITEMS, dtype=jnp.float32) / max(ITEMS - 1, 1)
    growth = 1.0 + 0.732 * position
    values = jax.random.normal(key_val, (ITEMS, R), jnp.float32)
    return values * column_scale[None, :] * growth[:, None] * R ** (-0.5)


def draw_user_gram(key, part):
    key_diag, key_off = jax.random.split(jax.random.fold_in(key, 23))
    diagonal = jnp.exp(jax.random.uniform(key_diag, (R,), jnp.float32, math.log(20.0), math.log(200.0)))
    noise = jax.random.uniform(key_off, (R, R), jnp.float32, -1.0, 1.0)
    symmetric = 0.5 * (noise + noise.T)
    smaller = jnp.minimum(diagonal[:, None], diagonal[None, :])
    offdiag = 0.3 * symmetric * smaller / R * (1.0 - jnp.eye(R, dtype=jnp.float32))
    return jnp.diag(diagonal) + offdiag


def draw_req_count(key, part):
    key_hot, key_pick, key_fill = jax.random.split(jax.random.fold_in(key, 37), 3)
    favored = jax.random.randint(key_pick, (), 0, NDEV)
    banded = jax.random.randint(key_hot, (NDEV,), 0, 4) == 0
    chosen = jnp.arange(NDEV, dtype=jnp.int32) == favored
    hotband = jnp.logical_or(banded, chosen)
    filled = jax.random.randint(key_fill, (NDEV, NDEV), 1, CAP + 1)
    return jnp.where(hotband[None, :], CAP, filled).astype(jnp.int32)


def set_ends(drawn, rng, low, top_value):
    spot = [jax.random.randint(jax.random.fold_in(rng, axis), (), 0, length) for axis, length in enumerate(drawn.shape)]
    widest = drawn.shape.index(max(drawn.shape))
    neighbour = spot[:widest] + [(spot[widest] + 1) % drawn.shape[widest]] + spot[widest + 1:]
    return drawn.at[tuple(spot)].set(low).at[tuple(neighbour)].set(top_value)


def level_of(own_key, dims, shards, least, high):
    level = 1.0
    for dim, parts in shards:
        steps = jax.random.uniform(jax.random.fold_in(jax.random.fold_in(own_key, 6), dim), (parts,), jnp.float32, least / len(shards), high / len(shards))
        level = level * jnp.repeat(jnp.exp(steps), dims[dim] // parts).reshape((-1,) + (1,) * (len(dims) - 1 - dim))
    return level


def scatter_about(rng, shape, width, limit, shards=(), kind=jnp.bfloat16):
    array = jax.random.normal(rng, shape, jnp.float32) * width
    if len(shards) > 0:
        array = level_of(rng, shape, shards, -0.22, 0.18) * array
    return jnp.clip(array, min=-limit, max=limit).astype(kind)


def setup_inputs(seed: int = 0) -> dict:
    arg_keys = jax.random.split(jax.random.key(seed), 10)
    return {
        "user_old": scatter_about(arg_keys[0], (USERS, R), 0.5, 3.0, ((0, 128),), jnp.float32),
        "item_old": draw_item_old(jax.random.fold_in(arg_keys[9], 71), 0),
        "item_rhs": scatter_about(arg_keys[2], (ITEMS, R), 60.0, 360.0, ((0, 128),), jnp.float32),
        "user_gram": draw_user_gram(jax.random.fold_in(arg_keys[9], 71), 0),
        "req_count": draw_req_count(jax.random.fold_in(arg_keys[9], 71), 0),
        "req_item": set_ends(jax.random.randint(arg_keys[5], (NDEV, NDEV, CAP), 0, ITEM_DEV), jax.random.fold_in(arg_keys[5], 1), 0, ITEM_DEV - 1).astype(jnp.int32),
        "req_user": set_ends(jax.random.randint(arg_keys[6], (NDEV, NDEV, CAP), 0, U_DEV), jax.random.fold_in(arg_keys[6], 1), 0, U_DEV - 1).astype(jnp.int32),
        "weight": jnp.clip(jnp.exp(math.log(20.0) - 2.9957323 * jax.random.uniform(arg_keys[7], (NDEV, NDEV, CAP), jnp.float32) ** level_of(arg_keys[7], (NDEV, NDEV, CAP), ((0, 128),), -0.2, 0.2)), 1.0, 20.0),
        "rating": scatter_about(arg_keys[8], (NDEV, NDEV, CAP), 1.0, 4.0, ((0, 128),), jnp.float32),
    }


ridge = 1.0
highest = lax.Precision.HIGHEST


def slot_terms(weight, rating, counts):
    slot_index = jnp.arange(weight.shape[-1], dtype=jnp.int32)
    live = slot_index < counts[..., None]
    weights = jnp.where(live, weight, 0.0)
    coefs = jnp.where(live, (1.0 + weight) * rating, 0.0)
    return weights, coefs


def refine(start, base, rows, targets, weights, coefs, gram):
    groups = start.shape[0]
    shifted = gram + ridge * jnp.eye(gram.shape[0], dtype=gram.dtype)

    def operate(vector):
        along = jnp.sum(rows * vector[targets], axis=1) * weights
        local_part = jnp.dot(vector, shifted, precision=highest)
        return local_part + jax.ops.segment_sum(along[:, None] * rows, targets, num_segments=groups)

    right = base + jax.ops.segment_sum(coefs[:, None] * rows, targets, num_segments=groups)
    resid = right - operate(start)
    direction = resid
    squares = jnp.sum(resid * resid, axis=1)
    solution = start
    for iteration in range(ITERS):
        image = operate(direction)
        alpha = squares / jnp.sum(direction * image, axis=1)
        solution = solution + alpha[:, None] * direction
        resid = resid - alpha[:, None] * image
        fresh = jnp.sum(resid * resid, axis=1)
        direction = resid + (fresh / squares)[:, None] * direction
        squares = fresh
    return solution


def reference(user_old, item_old, item_rhs, user_gram, req_count, req_item, req_user, weight, rating):
    rank = item_old.shape[1]
    weights, coefs = slot_terms(weight, rating, req_count)
    item_gram = jnp.dot(item_old.T, item_old, precision=highest)
    owner_base = (jnp.arange(NDEV, dtype=jnp.int32) * ITEM_DEV)[:, None]

    def user_side(packed):
        ids_item, ids_user, weight_dev, coef_dev, start = packed
        rows = item_old[(owner_base + ids_item).reshape(-1)]
        return refine(start, 0.0, rows, ids_user.reshape(-1), weight_dev.reshape(-1), coef_dev.reshape(-1), item_gram)

    user_new = lax.map(user_side, (req_item, req_user, weights, coefs, user_old.reshape(NDEV, U_DEV, rank)))
    user_new = user_new.reshape(USERS, rank)
    user_total = user_gram + jnp.dot(user_new.T, user_new, precision=highest)
    source_base = (jnp.arange(NDEV, dtype=jnp.int32) * U_DEV)[:, None]

    def item_side(packed):
        ids_item, ids_user, weight_own, coef_own, start, base = packed
        rows = user_new[(source_base + ids_user).reshape(-1)]
        return refine(start, base, rows, ids_item.reshape(-1), weight_own.reshape(-1), coef_own.reshape(-1), user_total)

    item_new = lax.map(item_side, (jnp.swapaxes(req_item, 0, 1), jnp.swapaxes(req_user, 0, 1), jnp.swapaxes(weights, 0, 1), jnp.swapaxes(coefs, 0, 1), item_old.reshape(NDEV, ITEM_DEV, rank), item_rhs.reshape(NDEV, ITEM_DEV, rank)))
    return user_new, item_new.reshape(ITEMS, rank)
```

```python
import functools
import jax
import jax.numpy as jnp
from jax import lax
from jax.sharding import PartitionSpec as P
from jax.experimental import pallas as pl
from jax.experimental.pallas import tpu as pltpu

ITERS = 8


ridge = 1.0
highest = lax.Precision.HIGHEST
MESH = pl.DeviceIdType.MESH


def slot_terms(weight, rating, counts):
    slot_index = jnp.arange(weight.shape[-1], dtype=jnp.int32)
    live = slot_index < counts[..., None]
    weights = jnp.where(live, weight, 0.0)
    coefs = jnp.where(live, (1.0 + weight) * rating, 0.0)
    return (weights, coefs)


def one_hot_table(targets, groups):
    return (targets[:, None] == jnp.arange(groups, dtype=jnp.int32)[None, :]).astype(jnp.float32)


def pick_rows(table, source):
    return jnp.dot(table, source, precision=highest)


def fold_rows(table, terms):
    return lax.dot_general(table, terms, (((0,), (0,)), ((), ())), precision=highest)


def refine(start, base, rows, targets, weights, coefs, gram):
    groups = start.shape[0]
    shifted = gram + ridge * jnp.eye(gram.shape[0], dtype=gram.dtype)
    table = one_hot_table(targets, groups)

    def operate(vector):
        along = jnp.sum(rows * pick_rows(table, vector), axis=1) * weights
        local_part = jnp.dot(vector, shifted, precision=highest)
        return local_part + fold_rows(table, along[:, None] * rows)

    right = base + fold_rows(table, coefs[:, None] * rows)
    resid = right - operate(start)
    direction = resid
    squares = jnp.sum(resid * resid, axis=1)
    solution = start
    for iteration in range(ITERS):
        image = operate(direction)
        alpha = squares / jnp.sum(direction * image, axis=1)
        solution = solution + alpha[:, None] * direction
        resid = resid - alpha[:, None] * image
        fresh = jnp.sum(resid * resid, axis=1)
        direction = resid + (fresh / squares)[:, None] * direction
        squares = fresh
    return solution


def exchange_kernel(n, fast, count, *refs):
    sources, targets = refs[:count], refs[count : 2 * count]
    send_sem, recv_sem, own_sem = refs[2 * count :]
    me = lax.axis_index("users") * fast + lax.axis_index("items")
    barrier = pltpu.get_barrier_semaphore()

    @pl.loop(1, n)
    def _(step):
        peer = lax.rem(me + step, n)
        pl.semaphore_signal(
            barrier, inc=1, device_id=(peer // fast, lax.rem(peer, fast)), device_id_type=MESH
        )

    pl.semaphore_wait(barrier, n - 1)

    def block(source, index):
        return source.at[index] if source.shape[0] == n else source.at[0]

    @pl.loop(1, n)
    def _(step):
        peer = lax.rem(me + step, n)
        for index, (source, target) in enumerate(zip(sources, targets)):
            pltpu.make_async_remote_copy(
                src_ref=block(source, peer),
                dst_ref=target.at[me],
                send_sem=send_sem.at[index],
                recv_sem=recv_sem.at[index],
                device_id=(peer // fast, lax.rem(peer, fast)),
                device_id_type=MESH,
            ).start()

    for index, (source, target) in enumerate(zip(sources, targets)):
        own = pltpu.make_async_copy(block(source, me), target.at[me], own_sem)
        own.start()
        own.wait()
    for index, target in enumerate(targets):
        span = target.at[pl.ds(0, n - 1)]
        pltpu.make_async_copy(span, span, send_sem.at[index]).wait()
        pltpu.make_async_copy(span, span, recv_sem.at[index]).wait()


def exchange(n, fast, which, *arrays):
    count = len(arrays)
    vmem = pl.BlockSpec(memory_space=pltpu.VMEM)
    return pl.pallas_call(
        functools.partial(exchange_kernel, n, fast, count),
        out_shape=tuple(jax.ShapeDtypeStruct((n,) + a.shape[1:], a.dtype) for a in arrays),
        in_specs=[vmem] * count,
        out_specs=(vmem,) * count,
        scratch_shapes=[
            pltpu.SemaphoreType.DMA((count,)),
            pltpu.SemaphoreType.DMA((count,)),
            pltpu.SemaphoreType.DMA,
        ],
        compiler_params=pltpu.CompilerParams(
            collective_id=which, has_side_effects=True, vmem_limit_bytes=32 * 2**20
        ),
    )(*arrays)


def per_device(
    user_old, item_old, item_rhs, user_gram, req_count, req_item, req_user, weight, rating
):
    fast = lax.axis_size("items")
    senders = lax.axis_size("users") * fast
    capacity = req_item.shape[2]
    rank = item_old.shape[1]
    weights, coefs = slot_terms(weight[0], rating[0], req_count[0])
    partial = jnp.dot(item_old.T, item_old, precision=highest)
    spare = jnp.zeros((senders, rank - 3 * capacity), jnp.float32)
    note = jnp.concatenate([req_item[0].astype(jnp.float32), weights, coefs, spare], axis=1)
    notes, parts = exchange(senders, fast, 0, note[:, None, :], partial[:, None, :])
    notes = notes[:, 0, :]
    asked_flat = notes[:, :capacity].astype(jnp.int32).reshape(-1)
    item_weights = notes[:, capacity : 2 * capacity].reshape(-1)
    item_coefs = notes[:, 2 * capacity : 3 * capacity].reshape(-1)
    gram_row = jnp.sum(parts, axis=0, keepdims=True)
    found = pick_rows(one_hot_table(asked_flat, item_old.shape[0]), item_old).reshape(
        senders, capacity, rank
    )
    fetched, item_gram = exchange(senders, fast, 1, found, gram_row)
    item_gram = item_gram[:, 0, :]
    fetched = fetched.reshape(senders * capacity, rank)
    members = req_user[0].reshape(-1)
    user_new = refine(
        user_old, 0.0, fetched, members, weights.reshape(-1), coefs.reshape(-1), item_gram
    )
    outgoing = pick_rows(one_hot_table(members, user_new.shape[0]), user_new).reshape(
        senders, capacity, rank
    )
    partial = jnp.dot(user_new.T, user_new, precision=highest)
    arrived, parts = exchange(senders, fast, 2, outgoing, partial[:, None, :])
    arrived = arrived.reshape(senders * capacity, rank)
    gram_row = jnp.sum(parts, axis=0, keepdims=True)
    (total,) = exchange(senders, fast, 3, gram_row)
    user_total = user_gram + total[:, 0, :]
    item_new = refine(
        item_old, item_rhs, arrived, asked_flat, item_weights, item_coefs, user_total
    )
    return (user_new, item_new)


def solution(mesh):
    in_specs = (
        P(("users", "items"), None),
        P(("users", "items"), None),
        P(("users", "items"), None),
        P(),
        P(("users", "items"), None),
        P(("users", "items"), None, None),
        P(("users", "items"), None, None),
        P(("users", "items"), None, None),
        P(("users", "items"), None, None),
    )
    out_specs = (P(("users", "items"), None), P(("users", "items"), None))
    return jax.shard_map(
        per_device, mesh=mesh, in_specs=in_specs, out_specs=out_specs, check_vma=False
    )
```

```python
import functools
import jax
import jax.numpy as jnp
from jax import lax
from jax.sharding import PartitionSpec as P
from jax.experimental import pallas as pl
from jax.experimental.pallas import tpu as pltpu

ITERS = 8
RIDGE = 1.0
CHUNK = 512
MESH = pl.DeviceIdType.MESH
F32 = jnp.float32
BF16 = jnp.bfloat16


def split2(value):
    high = value.astype(BF16)
    return high, (value - high.astype(F32)).astype(BF16)


def split3(value):
    high = value.astype(BF16)
    rest = value - high.astype(F32)
    middle = rest.astype(BF16)
    return high, middle, (rest - middle.astype(F32)).astype(BF16)


def dot(left, right):
    return jnp.dot(left, right, preferred_element_type=F32)


def halves(value):
    width = value.shape[1] // 2
    return value[:, :width] + value[:, width:]


def iota(shape, axis):
    return lax.broadcasted_iota(jnp.int32, shape, axis)


def owner_table(first, rows, capacity, senders):
    owner = lax.div(iota((rows, senders), 0), capacity) + first // capacity
    return (owner == iota((rows, senders), 1)).astype(F32).astype(BF16)


def spread(pieces, first, rows, capacity, senders):
    table = owner_table(first, rows, capacity, senders)
    wide = halves(dot(table, jnp.concatenate(pieces[:2], axis=1)))
    if len(pieces) > 2:
        wide = wide + dot(table, pieces[2])
    return wide


def column(wide, which, capacity):
    slot = lax.rem(iota(wide.shape, 0), capacity) + which * capacity
    return jnp.sum(jnp.where(slot == iota(wide.shape, 1), wide, 0.0), axis=1, keepdims=True)


def row_table(indices, groups, capacity, out):
    senders = indices.shape[1]
    both = jnp.concatenate(split2(indices), axis=0)
    slots = senders * capacity
    for first in range(0, slots, CHUNK):
        owner = lax.div(iota((senders, CHUNK), 1), capacity) + first // capacity
        table = (owner == iota((senders, CHUNK), 0)).astype(F32).astype(BF16)
        wide = dot(both, table)
        wide = wide[:capacity] + wide[capacity:]
        mine = iota(wide.shape, 0) == lax.rem(iota(wide.shape, 1), capacity)
        row = jnp.sum(jnp.where(mine, wide, 0.0), axis=0, keepdims=True).astype(jnp.int32)
        hot = (row == iota((groups, CHUNK), 0)).astype(F32).astype(BF16)
        out[:, pl.ds(first, CHUNK)] = hot


def column_table(wide, which, capacity, groups):
    index = column(wide, which, capacity).astype(jnp.int32)
    return (index == iota((wide.shape[0], groups), 1)).astype(F32).astype(BF16)


def set_gram(gram, pair, single):
    rank = gram.shape[0]
    ridge = jnp.where(iota((rank, rank), 0) == iota((rank, rank), 1), RIDGE, 0.0)
    high, middle, low = split3(gram + ridge)
    pair[...] = jnp.concatenate(
        [jnp.concatenate([high, middle], axis=1), jnp.concatenate([middle, high], axis=1)], axis=0
    )
    single[...] = jnp.concatenate([low, high], axis=0)


def gram_product(vector, pair, single):
    high, middle, low = split3(vector)
    first = dot(jnp.concatenate([high, middle], axis=1), pair[...])
    return halves(first) + dot(jnp.concatenate([high, low], axis=1), single[...])


def slot_pass(vector, rows_ref, scaled, coefs, hot, hot_t):
    slots, rank = scaled.shape
    capacity = rows_ref.shape[1]
    pieces = jnp.concatenate(split2(vector), axis=1)
    total = None
    for first in range(0, slots, CHUNK):
        part = pl.ds(first, CHUNK)
        rows = rows_ref[pl.ds(first // capacity, CHUNK // capacity)].reshape(CHUNK, rank)
        along = jnp.sum(rows * halves(dot(hot[part, :], pieces)), axis=1, keepdims=True)
        if coefs is None:
            terms = along * scaled[part, :]
        else:
            weighted = scaled[part, :] * rows
            scaled[part, :] = weighted
            terms = coefs[part, :] * rows - along * weighted
        folded = dot(hot_t[:, part], jnp.concatenate(split2(terms), axis=1))
        total = folded if total is None else total + folded
    return halves(total)


def conjugate_steps(x_ref, resid, direction, operate):
    def step(iteration, squares):
        p = direction[...]
        image = operate(p)
        alpha = squares / jnp.sum(p * image, axis=1, keepdims=True)
        x_ref[...] = x_ref[...] + alpha * p
        r = resid[...] - alpha * image
        resid[...] = r
        fresh = jnp.sum(r * r, axis=1, keepdims=True)
        direction[...] = r + (fresh / squares) * p
        return fresh

    r = resid[...]
    direction[...] = r
    lax.fori_loop(0, ITERS, step, jnp.sum(r * r, axis=1, keepdims=True))


def body(
    n,
    fast,
    capacity,
    user_hbm,
    item_hbm,
    rhs_hbm,
    user_gram,
    req_count,
    req_item,
    req_user,
    weight,
    rating,
    user_out,
    item_out,
    user_v,
    item_v,
    rhs_v,
    note_src,
    notes,
    part_src,
    parts,
    row_src,
    gram_rows,
    part2_src,
    parts2,
    row2_src,
    gram2_rows,
    found,
    fetched,
    outgoing,
    arrived,
    user_scaled,
    user_coefs,
    item_scaled,
    item_coefs,
    user_hot,
    user_hot_t,
    item_hot,
    item_hot_t,
    pair,
    single,
    user_r,
    user_p,
    item_r,
    item_p,
    send_sem,
    recv_sem,
    own_sem,
    load_sem,
):
    me = lax.axis_index("users") * fast + lax.axis_index("items")
    slots = n * capacity
    rank = user_out.shape[1]
    users, items = user_out.shape[0], item_out.shape[0]
    barrier = pltpu.get_barrier_semaphore()

    loads = [
        pltpu.make_async_copy(source, target, load_sem.at[index])
        for index, (source, target) in enumerate(
            ((item_hbm, item_v), (user_hbm, user_v), (rhs_hbm, rhs_v))
        )
    ]
    for load in loads:
        load.start()

    def place(step):
        peer = lax.rem(me + step, n)
        return peer, (lax.div(peer, fast), lax.rem(peer, fast))

    @pl.loop(1, n)
    def _(step):
        _, device = place(step)
        pl.semaphore_signal(barrier, inc=1, device_id=device, device_id_type=MESH)

    def block(source, index):
        return source.at[index] if source.shape[0] == n else source.at[0]

    def send(which, source, target):
        @pl.loop(1, n)
        def _(step):
            peer, device = place(step)
            pltpu.make_async_remote_copy(
                src_ref=block(source, peer),
                dst_ref=target.at[me],
                send_sem=send_sem.at[which],
                recv_sem=recv_sem.at[which],
                device_id=device,
                device_id_type=MESH,
            ).start()

        pltpu.make_async_copy(block(source, me), target.at[me], own_sem.at[which]).start()

    def arrive(which, source, target):
        span = target.at[pl.ds(0, n - 1)]
        pltpu.make_async_copy(span, span, recv_sem.at[which]).wait()
        pltpu.make_async_copy(block(source, me), target.at[me], own_sem.at[which]).wait()

    def sent(which, target):
        span = target.at[pl.ds(0, n - 1)]
        pltpu.make_async_copy(span, span, send_sem.at[which]).wait()

    live = iota((capacity, n), 0) < req_count[...]
    weights = jnp.where(live, weight[...], 0.0)
    coefs = jnp.where(live, (1.0 + weight[...]) * rating[...], 0.0)
    asked = req_item[...].astype(F32)
    members = req_user[...].astype(F32)
    rest = jnp.zeros((rank - 4 * capacity, n), F32)
    own_note = jnp.concatenate([asked, weights, coefs, members, rest], axis=0).T
    note_src[...] = own_note[:, None, :]
    pl.semaphore_wait(barrier, n - 1)
    send(0, note_src, notes)

    loads[0].wait()
    mine = item_v[...]
    partial = jnp.dot(mine.T, mine, precision=lax.Precision.HIGHEST, preferred_element_type=F32)
    part_src[...] = partial[:, None, :]
    send(1, part_src, parts)

    pieces = split3(own_note)
    for first in range(0, slots, CHUNK):
        part = pl.ds(first, CHUNK)
        wide = spread(pieces, first, CHUNK, capacity, n)
        user_scaled[part, :] = jnp.broadcast_to(column(wide, 1, capacity), (CHUNK, rank))
        user_coefs[part, :] = jnp.broadcast_to(column(wide, 2, capacity), (CHUNK, rank))
        user_hot[part, :] = column_table(wide, 3, capacity, users)
    row_table(members, users, capacity, user_hot_t)

    arrive(0, note_src, notes)
    all_notes = notes[:, 0, :]
    pieces = split3(all_notes)
    item_pieces = split3(item_v[...])
    item_pair = jnp.concatenate(item_pieces[:2], axis=1)
    for first in range(0, slots, CHUNK):
        part = pl.ds(first, CHUNK)
        wide = spread(pieces[:2], first, CHUNK, capacity, n)
        hot = column_table(wide, 0, capacity, items)
        item_hot[part, :] = hot
        picked = halves(dot(hot, item_pair)) + dot(hot, item_pieces[2])
        found[pl.ds(first // capacity, CHUNK // capacity)] = picked.reshape(
            CHUNK // capacity, capacity, rank
        )
    send(2, found, fetched)
    arrive(1, part_src, parts)
    row_src[...] = jnp.sum(parts[...], axis=0, keepdims=True)
    send(3, row_src, gram_rows)

    for first in range(0, slots, CHUNK):
        part = pl.ds(first, CHUNK)
        wide = spread(pieces, first, CHUNK, capacity, n)
        item_scaled[part, :] = jnp.broadcast_to(column(wide, 1, capacity), (CHUNK, rank))
        item_coefs[part, :] = jnp.broadcast_to(column(wide, 2, capacity), (CHUNK, rank))
    row_table(all_notes.T[:capacity], items, capacity, item_hot_t)

    loads[1].wait()
    arrive(2, found, fetched)
    start = user_v[...]
    right = slot_pass(start, fetched, user_scaled, user_coefs, user_hot, user_hot_t)
    arrive(3, row_src, gram_rows)
    set_gram(gram_rows[:, 0, :], pair, single)
    user_r[...] = right - gram_product(start, pair, single)
    user_v[...] = start

    def user_operate(vector):
        return gram_product(vector, pair, single) + slot_pass(
            vector, fetched, user_scaled, None, user_hot, user_hot_t
        )

    conjugate_steps(user_v, user_r, user_p, user_operate)
    refreshed = user_v[...]
    user_out[...] = refreshed

    partial = jnp.dot(
        refreshed.T, refreshed, precision=lax.Precision.HIGHEST, preferred_element_type=F32
    )
    part2_src[...] = partial[:, None, :]
    send(4, part2_src, parts2)
    user_pieces = split3(refreshed)
    user_pair = jnp.concatenate(user_pieces[:2], axis=1)
    for first in range(0, slots, CHUNK):
        hot = user_hot[pl.ds(first, CHUNK), :]
        picked = halves(dot(hot, user_pair)) + dot(hot, user_pieces[2])
        outgoing[pl.ds(first // capacity, CHUNK // capacity)] = picked.reshape(
            CHUNK // capacity, capacity, rank
        )
    send(5, outgoing, arrived)
    arrive(4, part2_src, parts2)
    row2_src[...] = jnp.sum(parts2[...], axis=0, keepdims=True)
    send(6, row2_src, gram2_rows)

    loads[2].wait()
    arrive(5, outgoing, arrived)
    start = item_v[...]
    right = rhs_v[...] + slot_pass(
        start, arrived, item_scaled, item_coefs, item_hot, item_hot_t
    )
    arrive(6, row2_src, gram2_rows)
    set_gram(user_gram[...] + gram2_rows[:, 0, :], pair, single)
    item_r[...] = right - gram_product(start, pair, single)
    item_out[...] = start

    def item_operate(vector):
        return gram_product(vector, pair, single) + slot_pass(
            vector, arrived, item_scaled, None, item_hot, item_hot_t
        )

    conjugate_steps(item_out, item_r, item_p, item_operate)
    for which, target in enumerate(
        (notes, parts, fetched, gram_rows, parts2, arrived, gram2_rows)
    ):
        sent(which, target)


def per_device(
    user_old, item_old, item_rhs, user_gram, req_count, req_item, req_user, weight, rating
):
    fast = lax.axis_size("items")
    n = lax.axis_size("users") * fast
    capacity = req_item.shape[2]
    users, rank = user_old.shape
    items = item_old.shape[0]
    slots = n * capacity
    vmem = pl.BlockSpec(memory_space=pltpu.VMEM)
    anywhere = pl.BlockSpec(memory_space=pl.ANY)
    row = pltpu.VMEM((1, 1, rank), F32)
    rows = pltpu.VMEM((n, 1, rank), F32)
    factors = pltpu.VMEM((n, capacity, rank), F32)
    scaled = pltpu.VMEM((slots, rank), F32)
    flip = lambda array: jnp.swapaxes(array[0], 0, 1)
    return pl.pallas_call(
        functools.partial(body, n, fast, capacity),
        out_shape=(
            jax.ShapeDtypeStruct((users, rank), F32),
            jax.ShapeDtypeStruct((items, rank), F32),
        ),
        in_specs=[anywhere] * 3 + [vmem] * 6,
        out_specs=(vmem, vmem),
        scratch_shapes=[
            pltpu.VMEM((users, rank), F32),
            pltpu.VMEM((items, rank), F32),
            pltpu.VMEM((items, rank), F32),
            rows,
            rows,
            rows,
            rows,
            row,
            rows,
            rows,
            rows,
            row,
            rows,
            factors,
            factors,
            factors,
            factors,
            scaled,
            scaled,
            scaled,
            scaled,
            pltpu.VMEM((slots, users), BF16),
            pltpu.VMEM((users, slots), BF16),
            pltpu.VMEM((slots, items), BF16),
            pltpu.VMEM((items, slots), BF16),
            pltpu.VMEM((2 * rank, 2 * rank), BF16),
            pltpu.VMEM((2 * rank, rank), BF16),
            pltpu.VMEM((users, rank), F32),
            pltpu.VMEM((users, rank), F32),
            pltpu.VMEM((items, rank), F32),
            pltpu.VMEM((items, rank), F32),
            pltpu.SemaphoreType.DMA((7,)),
            pltpu.SemaphoreType.DMA((7,)),
            pltpu.SemaphoreType.DMA((7,)),
            pltpu.SemaphoreType.DMA((3,)),
        ],
        compiler_params=pltpu.CompilerParams(
            collective_id=0, has_side_effects=True, vmem_limit_bytes=40 * 2**20
        ),
    )(
        user_old,
        item_old,
        item_rhs,
        user_gram,
        req_count,
        flip(req_item),
        flip(req_user),
        flip(weight),
        flip(rating),
    )


def solution(mesh):
    in_specs = (
        P(("users", "items"), None),
        P(("users", "items"), None),
        P(("users", "items"), None),
        P(),
        P(("users", "items"), None),
        P(("users", "items"), None, None),
        P(("users", "items"), None, None),
        P(("users", "items"), None, None),
        P(("users", "items"), None, None),
    )
    out_specs = (P(("users", "items"), None), P(("users", "items"), None))
    return jax.shard_map(
        per_device, mesh=mesh, in_specs=in_specs, out_specs=out_specs, check_vma=False
    )
```

```python
import functools
from typing import Any, NamedTuple
import jax
import jax.numpy as jnp
from jax import lax
from jax.sharding import PartitionSpec as P
from jax.experimental import pallas as pl
from jax.experimental.pallas import tpu as pltpu

ITERS = 8
RIDGE = 1.0
CHUNK = 512
PICK = 128
MESH = pl.DeviceIdType.MESH
F32 = jnp.float32
BF16 = jnp.bfloat16


def split2(value):
    high = value.astype(BF16)
    return high, (value - high.astype(F32)).astype(BF16)


def split3(value):
    high = value.astype(BF16)
    rest = value - high.astype(F32)
    middle = rest.astype(BF16)
    return high, middle, (rest - middle.astype(F32)).astype(BF16)


def dot(left, right):
    return jnp.dot(left, right, preferred_element_type=F32)


def halves(value):
    width = value.shape[1] // 2
    return value[:, :width] + value[:, width:]


def iota(shape, axis):
    return lax.broadcasted_iota(jnp.int32, shape, axis)


def owner_table(first, rows, capacity, senders):
    owner = lax.div(iota((rows, senders), 0), capacity) + first
    return (owner == iota((rows, senders), 1)).astype(F32).astype(BF16)


def spread(pieces, first, rows, capacity, senders):
    table = owner_table(first, rows, capacity, senders)
    wide = halves(dot(table, jnp.concatenate(pieces[:2], axis=1)))
    if len(pieces) > 2:
        wide = wide + dot(table, pieces[2])
    return wide


def column(wide, which, capacity):
    slot = lax.rem(iota(wide.shape, 0), capacity) + which * capacity
    return jnp.sum(jnp.where(slot == iota(wide.shape, 1), wide, 0.0), axis=1, keepdims=True)


def row_table(indices, groups, capacity, out):
    senders = indices.shape[1]
    both = jnp.concatenate(split2(indices), axis=0)
    slots = senders * capacity
    for first in range(0, slots, CHUNK):
        owner = lax.div(iota((senders, CHUNK), 1), capacity) + first // capacity
        table = (owner == iota((senders, CHUNK), 0)).astype(F32).astype(BF16)
        wide = dot(both, table)
        wide = wide[:capacity] + wide[capacity:]
        mine = iota(wide.shape, 0) == lax.rem(iota(wide.shape, 1), capacity)
        row = jnp.sum(jnp.where(mine, wide, 0.0), axis=0, keepdims=True).astype(jnp.int32)
        hot = (row == iota((groups, CHUNK), 0)).astype(F32).astype(BF16)
        out[:, pl.ds(first, CHUNK)] = hot


def column_table(wide, which, capacity, groups):
    index = column(wide, which, capacity).astype(jnp.int32)
    return (index == iota((wide.shape[0], groups), 1)).astype(F32).astype(BF16)


def set_gram(gram, pair, single):
    rank = gram.shape[0]
    ridge = jnp.where(iota((rank, rank), 0) == iota((rank, rank), 1), RIDGE, 0.0)
    high, middle, low = split3(gram + ridge)
    pair[...] = jnp.concatenate(
        [jnp.concatenate([high, middle], axis=1), jnp.concatenate([middle, high], axis=1)], axis=0
    )
    single[...] = jnp.concatenate([low, high], axis=0)


class State(NamedTuple):
    x: Any
    r: Any
    p: Any
    squares: Any
    pieces: Any
    terms: Any
    pair: Any
    single: Any
    block: int


def pick_terms(state, rows_ref, scaled, coefs, hot):
    slots, rank = scaled.shape
    capacity = rows_ref.shape[1]
    for first in range(0, slots, PICK):
        part = pl.ds(first, PICK)
        rows = rows_ref[pl.ds(first // capacity, PICK // capacity)].reshape(PICK, rank)
        picked = halves(dot(hot[part, :], state.pieces[:, : 2 * rank]))
        along = jnp.sum(rows * picked, axis=1, keepdims=True)
        if coefs is None:
            terms = along * scaled[part, :]
        else:
            weighted = scaled[part, :] * rows
            scaled[part, :] = weighted
            terms = coefs[part, :] * rows - along * weighted
        high, low = split2(terms)
        state.terms[part, :rank] = high
        state.terms[part, rank:] = low


def keep_pieces(state, part, value):
    rank = value.shape[1]
    for index, piece in enumerate(split3(value)):
        state.pieces[part, index * rank : (index + 1) * rank] = piece


def gram_part(state, part, rank):
    mine = state.pieces[part, :]
    first = dot(mine[:, : 2 * rank], state.pair[...])
    outer = jnp.concatenate([mine[:, :rank], mine[:, 2 * rank :]], axis=1)
    return halves(first) + dot(outer, state.single[...])


def begin(state, rows_ref, scaled, coefs, hot):
    keep_pieces(state, slice(None), state.x[...])
    pick_terms(state, rows_ref, scaled, coefs, hot)


def conjugate_steps(state, base, rows_ref, scaled, hot, hot_t):
    groups, rank = state.x.shape
    for first in range(0, groups, state.block):
        part = pl.ds(first, state.block)
        r = halves(dot(hot_t[part, :], state.terms[...])) - gram_part(state, part, rank)
        if base is not None:
            r = r + base[part, :]
        state.r[part, :] = r
        state.p[part, :] = r
        squares = jnp.sum(r * r, axis=1, keepdims=True)
        state.squares[part, :] = jnp.broadcast_to(squares, r.shape)
    keep_pieces(state, slice(None), state.p[...])

    def step(iteration, carry):
        pick_terms(state, rows_ref, scaled, None, hot)
        for first in range(0, groups, state.block):
            part = pl.ds(first, state.block)
            image = halves(dot(hot_t[part, :], state.terms[...])) + gram_part(state, part, rank)
            p = state.p[part, :]
            squares = state.squares[part, :]
            alpha = squares / jnp.sum(p * image, axis=1, keepdims=True)
            state.x[part, :] = state.x[part, :] + alpha * p
            r = state.r[part, :] - alpha * image
            state.r[part, :] = r
            fresh = jnp.sum(r * r, axis=1, keepdims=True)
            p = r + (fresh / squares) * p
            state.p[part, :] = p
            state.squares[part, :] = jnp.broadcast_to(fresh, p.shape)
            keep_pieces(state, part, p)
        return carry

    lax.fori_loop(0, ITERS, step, 0)


def body(
    n,
    fast,
    capacity,
    user_in,
    item_in,
    rhs_in,
    user_gram_in,
    count_in,
    asked_in,
    members_in,
    weight_in,
    rating_in,
    user_out,
    item_out,
    item_v,
    rhs_v,
    user_gram,
    count_v,
    asked_v,
    members_v,
    weight_v,
    rating_v,
    note_src,
    notes,
    partial,
    near,
    across,
    whole,
    partial2,
    near2,
    across2,
    whole2,
    found,
    fetched,
    outgoing,
    arrived,
    user_scaled,
    user_coefs,
    item_scaled,
    item_coefs,
    user_hot,
    user_hot_t,
    item_hot,
    item_hot_t,
    pair,
    single,
    terms,
    user_r,
    user_p,
    user_squares,
    user_pieces,
    item_r,
    item_p,
    item_squares,
    item_pieces,
    send_sem,
    recv_sem,
    own_sem,
    load_sem,
):
    me = lax.axis_index("users") * fast + lax.axis_index("items")
    slots = n * capacity
    users, rank = user_out.shape
    items = item_out.shape[0]
    inner = near.shape[0]
    outer = across.shape[0]
    band = rank // inner
    seat, team = lax.rem(me, inner), lax.div(me, inner)
    region = CHUNK // capacity
    barrier = pltpu.get_barrier_semaphore()

    loads = [
        pltpu.make_async_copy(source, target, load_sem.at[index])
        for index, (source, target) in enumerate(
            (
                (count_in, count_v),
                (asked_in, asked_v),
                (members_in, members_v),
                (weight_in, weight_v),
                (rating_in, rating_v),
                (item_in, item_v),
                (user_in, user_out),
                (rhs_in, rhs_v),
                (user_gram_in, user_gram),
                (item_in, item_out),
            )
        )
    ]
    for load in loads:
        load.start()

    def at(peer):
        return (lax.div(peer, fast), lax.rem(peer, fast))

    @pl.loop(1, n)
    def _(step):
        pl.semaphore_signal(
            barrier, inc=1, device_id=at(lax.rem(me + step, n)), device_id_type=MESH
        )

    def push(which, source, target, peer):
        pltpu.make_async_remote_copy(
            src_ref=source,
            dst_ref=target,
            send_sem=send_sem.at[which],
            recv_sem=recv_sem.at[which],
            device_id=at(peer),
            device_id_type=MESH,
        ).start()

    def landed(which, target):
        span = target.at[pl.ds(0, target.shape[0] - 1)]
        pltpu.make_async_copy(span, span, recv_sem.at[which]).wait()

    def sent(which, target):
        span = target.at[pl.ds(0, target.shape[0] - 1)]
        pltpu.make_async_copy(span, span, send_sem.at[which]).wait()

    def own(which, source, target):
        return pltpu.make_async_copy(source.at[me], target.at[me], own_sem.at[which])

    def gram_near(which, source, first):
        first[seat] = source[pl.ds(pl.multiple_of(seat * band, band), band), :]

        @pl.loop(1, inner)
        def _(step):
            other = lax.rem(seat + step, inner)
            push(
                which,
                source.at[pl.ds(pl.multiple_of(other * band, band), band)],
                first.at[seat],
                team * inner + other,
            )

    def gram_across(which, first, second):
        landed(which, first)
        second[team] = jnp.sum(first[...], axis=0)

        @pl.loop(1, outer)
        def _(step):
            other = lax.rem(team + step, outer)
            push(which + 1, second.at[team], second.at[team], other * inner + seat)

    def gram_back(which, second, third):
        landed(which + 1, second)
        third[seat] = jnp.sum(second[...], axis=0)

        @pl.loop(1, inner)
        def _(step):
            other = lax.rem(seat + step, inner)
            push(which + 2, third.at[seat], third.at[seat], team * inner + other)

    def gram_value(which, third):
        landed(which + 2, third)
        return third[...].reshape(rank, rank)

    def send_region(which, source, target, base):
        @pl.loop(0, region)
        def _(step):
            peer = base + lax.rem(me + step, region)

            @pl.when(peer != me)
            def _():
                push(which, source.at[peer], target.at[me], peer)

    def turn(step):
        return lax.rem(lax.axis_index("items") + step, slots // CHUNK)

    for load in loads[:5]:
        load.wait()
    live = iota((capacity, n), 0) < count_v[...]
    weights = jnp.where(live, weight_v[...], 0.0)
    coefs = jnp.where(live, (1.0 + weight_v[...]) * rating_v[...], 0.0)
    asked = asked_v[...].astype(F32)
    members = members_v[...].astype(F32)
    rest = jnp.zeros((rank - 4 * capacity, n), F32)
    own_note = jnp.concatenate([asked, weights, coefs, members, rest], axis=0).T
    note_src[...] = own_note[:, None, :]
    loads[5].wait()
    mine = item_v[...]
    partial[...] = jnp.dot(
        mine.T, mine, precision=lax.Precision.HIGHEST, preferred_element_type=F32
    )
    pl.semaphore_wait(barrier, n - 1)

    @pl.loop(1, n)
    def _(step):
        peer = lax.rem(me + step, n)
        push(0, note_src.at[peer], notes.at[me], peer)

    own(0, note_src, notes).start()
    gram_near(3, partial, near)

    pieces = split3(own_note)
    for first in range(0, slots, CHUNK):
        part = pl.ds(first, CHUNK)
        wide = spread(pieces, first // capacity, CHUNK, capacity, n)
        user_scaled[part, :] = jnp.broadcast_to(column(wide, 1, capacity), (CHUNK, rank))
        user_coefs[part, :] = jnp.broadcast_to(column(wide, 2, capacity), (CHUNK, rank))
        user_hot[part, :] = column_table(wide, 3, capacity, users)
    gram_across(3, near, across)
    row_table(members, users, capacity, user_hot_t)

    own(0, note_src, notes).wait()
    landed(0, notes)
    all_notes = notes[:, 0, :]
    pieces = split3(all_notes)
    item_split = split3(item_v[...])
    item_pair = jnp.concatenate(item_split[:2], axis=1)
    for step in range(slots // CHUNK):
        base = pl.multiple_of(turn(step) * region, region)
        wide = spread(pieces[:2], base, CHUNK, capacity, n)
        hot = column_table(wide, 0, capacity, items)
        item_hot[pl.ds(pl.multiple_of(base * capacity, CHUNK), CHUNK), :] = hot
        picked = halves(dot(hot, item_pair)) + dot(hot, item_split[2])
        found[pl.ds(base, region)] = picked.reshape(region, capacity, rank)
        send_region(1, found, fetched, base)
        if step == 0:
            gram_back(3, across, whole)
    own(1, found, fetched).start()

    for first in range(0, slots, CHUNK):
        part = pl.ds(first, CHUNK)
        wide = spread(pieces, first // capacity, CHUNK, capacity, n)
        item_scaled[part, :] = jnp.broadcast_to(column(wide, 1, capacity), (CHUNK, rank))
        item_coefs[part, :] = jnp.broadcast_to(column(wide, 2, capacity), (CHUNK, rank))
    row_table(all_notes.T[:capacity], items, capacity, item_hot_t)

    loads[6].wait()
    state = State(
        user_out, user_r, user_p, user_squares, user_pieces, terms, pair, single, users // 2
    )
    own(1, found, fetched).wait()
    landed(1, fetched)
    begin(state, fetched, user_scaled, user_coefs, user_hot)
    set_gram(gram_value(3, whole), pair, single)
    conjugate_steps(state, None, fetched, user_scaled, user_hot, user_hot_t)

    refreshed = user_out[...]
    partial2[...] = jnp.dot(
        refreshed.T, refreshed, precision=lax.Precision.HIGHEST, preferred_element_type=F32
    )
    gram_near(6, partial2, near2)
    user_split = split3(refreshed)
    user_pair = jnp.concatenate(user_split[:2], axis=1)
    for step in range(slots // CHUNK):
        base = pl.multiple_of(turn(step) * region, region)
        hot = user_hot[pl.ds(pl.multiple_of(base * capacity, CHUNK), CHUNK), :]
        picked = halves(dot(hot, user_pair)) + dot(hot, user_split[2])
        outgoing[pl.ds(base, region)] = picked.reshape(region, capacity, rank)
        send_region(2, outgoing, arrived, base)
        if step == 1:
            gram_across(6, near2, across2)
        if step == 2:
            gram_back(6, across2, whole2)
    own(2, outgoing, arrived).start()

    for load in loads[7:]:
        load.wait()
    state = State(
        item_out, item_r, item_p, item_squares, item_pieces, terms, pair, single, items // 2
    )
    set_gram(user_gram[...] + gram_value(6, whole2), pair, single)
    own(2, outgoing, arrived).wait()
    landed(2, arrived)
    begin(state, arrived, item_scaled, item_coefs, item_hot)
    conjugate_steps(state, rhs_v, arrived, item_scaled, item_hot, item_hot_t)
    for which, target in enumerate(
        (notes, fetched, arrived, near, across, whole, near2, across2, whole2)
    ):
        sent(which, target)


def per_device(
    user_old, item_old, item_rhs, user_gram, req_count, req_item, req_user, weight, rating
):
    fast = lax.axis_size("items")
    n = lax.axis_size("users") * fast
    capacity = req_item.shape[2]
    users, rank = user_old.shape
    items = item_old.shape[0]
    slots = n * capacity
    inner = 2 * fast
    outer = n // inner
    vmem = pl.BlockSpec(memory_space=pltpu.VMEM)
    hbm = pl.BlockSpec(memory_space=pltpu.HBM)

    def floats(*shape):
        return pltpu.VMEM(shape, F32)

    gram = [
        floats(rank, rank),
        floats(inner, rank // inner, rank),
        floats(outer, rank // inner, rank),
        floats(inner, rank // inner, rank),
    ]
    flip = lambda array: jnp.swapaxes(array[0], 0, 1)
    return pl.pallas_call(
        functools.partial(body, n, fast, capacity),
        out_shape=(
            jax.ShapeDtypeStruct((users, rank), F32),
            jax.ShapeDtypeStruct((items, rank), F32),
        ),
        in_specs=[hbm] * 9,
        out_specs=(vmem, vmem),
        scratch_shapes=[
            floats(items, rank),
            floats(items, rank),
            floats(rank, rank),
            pltpu.VMEM((1, n), jnp.int32),
            pltpu.VMEM((capacity, n), jnp.int32),
            pltpu.VMEM((capacity, n), jnp.int32),
            floats(capacity, n),
            floats(capacity, n),
            floats(n, 1, rank),
            floats(n, 1, rank),
            *gram,
            *gram,
            *[floats(n, capacity, rank)] * 4,
            *[floats(slots, rank)] * 4,
            pltpu.VMEM((slots, users), BF16),
            pltpu.VMEM((users, slots), BF16),
            pltpu.VMEM((slots, items), BF16),
            pltpu.VMEM((items, slots), BF16),
            pltpu.VMEM((2 * rank, 2 * rank), BF16),
            pltpu.VMEM((2 * rank, rank), BF16),
            pltpu.VMEM((slots, 2 * rank), BF16),
            *[floats(users, rank)] * 3,
            pltpu.VMEM((users, 3 * rank), BF16),
            *[floats(items, rank)] * 3,
            pltpu.VMEM((items, 3 * rank), BF16),
            pltpu.SemaphoreType.DMA((9,)),
            pltpu.SemaphoreType.DMA((9,)),
            pltpu.SemaphoreType.DMA((3,)),
            pltpu.SemaphoreType.DMA((10,)),
        ],
        compiler_params=pltpu.CompilerParams(
            collective_id=0, has_side_effects=True, vmem_limit_bytes=60 * 2**20
        ),
    )(
        user_old,
        item_old,
        item_rhs,
        user_gram,
        req_count,
        flip(req_item),
        flip(req_user),
        flip(weight),
        flip(rating),
    )


def solution(mesh):
    in_specs = (
        P(("users", "items"), None),
        P(("users", "items"), None),
        P(("users", "items"), None),
        P(),
        P(("users", "items"), None),
        P(("users", "items"), None, None),
        P(("users", "items"), None, None),
        P(("users", "items"), None, None),
        P(("users", "items"), None, None),
    )
    out_specs = (P(("users", "items"), None), P(("users", "items"), None))
    return jax.shard_map(
        per_device, mesh=mesh, in_specs=in_specs, out_specs=out_specs, check_vma=False
    )
```

```python
import functools
from typing import Any, NamedTuple
import jax
import jax.numpy as jnp
from jax import lax
from jax.sharding import PartitionSpec as P
from jax.experimental import pallas as pl
from jax.experimental.pallas import tpu as pltpu

ITERS = 8
RIDGE = 1.0
CHUNK = 512
PICK = 128
MESH = pl.DeviceIdType.MESH
F32 = jnp.float32
BF16 = jnp.bfloat16


def split2(value):
    high = value.astype(BF16)
    return high, (value - high.astype(F32)).astype(BF16)


def split3(value):
    high = value.astype(BF16)
    rest = value - high.astype(F32)
    middle = rest.astype(BF16)
    return high, middle, (rest - middle.astype(F32)).astype(BF16)


def dot(left, right):
    return jnp.dot(left, right, preferred_element_type=F32)


def halves(value):
    width = value.shape[1] // 2
    return value[:, :width] + value[:, width:]


def iota(shape, axis):
    return lax.broadcasted_iota(jnp.int32, shape, axis)


def owner_table(first, rows, capacity, senders):
    owner = lax.div(iota((rows, senders), 0), capacity) + first
    return (owner == iota((rows, senders), 1)).astype(F32).astype(BF16)


def spread(pieces, first, rows, capacity, senders):
    table = owner_table(first, rows, capacity, senders)
    wide = halves(dot(table, jnp.concatenate(pieces[:2], axis=1)))
    if len(pieces) > 2:
        wide = wide + dot(table, pieces[2])
    return wide


def column(wide, which, capacity):
    slot = lax.rem(iota(wide.shape, 0), capacity) + which * capacity
    return jnp.sum(jnp.where(slot == iota(wide.shape, 1), wide, 0.0), axis=1, keepdims=True)


def row_table(indices, groups, capacity, out):
    senders = indices.shape[1]
    both = jnp.concatenate(split2(indices), axis=0)
    slots = senders * capacity
    for first in range(0, slots, CHUNK):
        owner = lax.div(iota((senders, CHUNK), 1), capacity) + first // capacity
        table = (owner == iota((senders, CHUNK), 0)).astype(F32).astype(BF16)
        wide = dot(both, table)
        wide = wide[:capacity] + wide[capacity:]
        mine = iota(wide.shape, 0) == lax.rem(iota(wide.shape, 1), capacity)
        row = jnp.sum(jnp.where(mine, wide, 0.0), axis=0, keepdims=True).astype(jnp.int32)
        hot = (row == iota((groups, CHUNK), 0)).astype(F32).astype(BF16)
        out[:, pl.ds(first, CHUNK)] = hot


def column_table(wide, which, capacity, groups):
    index = column(wide, which, capacity).astype(jnp.int32)
    return (index == iota((wide.shape[0], groups), 1)).astype(F32).astype(BF16)


def set_gram(gram, pair, single):
    rank = gram.shape[0]
    ridge = jnp.where(iota((rank, rank), 0) == iota((rank, rank), 1), RIDGE, 0.0)
    high, middle, low = split3(gram + ridge)
    pair[...] = jnp.concatenate(
        [jnp.concatenate([high, middle], axis=1), jnp.concatenate([middle, high], axis=1)], axis=0
    )
    single[...] = jnp.concatenate([low, high], axis=0)


class State(NamedTuple):
    x: Any
    r: Any
    p: Any
    squares: Any
    pieces: Any
    terms: Any
    pair: Any
    single: Any
    block: int


def pick_terms(state, rows_ref, scaled, coefs, hot):
    slots, rank = scaled.shape
    capacity = rows_ref.shape[1]
    for first in range(0, slots, PICK):
        part = pl.ds(first, PICK)
        rows = rows_ref[pl.ds(first // capacity, PICK // capacity)].reshape(PICK, rank)
        picked = halves(dot(hot[part, :], state.pieces[:, : 2 * rank]))
        along = jnp.sum(rows * picked, axis=1, keepdims=True)
        if coefs is None:
            terms = along * scaled[part, :]
        else:
            weighted = scaled[part, :] * rows
            scaled[part, :] = weighted
            terms = coefs[part, :] * rows - along * weighted
        high, low = split2(terms)
        state.terms[part, :rank] = high
        state.terms[part, rank:] = low


def keep_pieces(state, part, value):
    rank = value.shape[1]
    for index, piece in enumerate(split3(value)):
        state.pieces[part, index * rank : (index + 1) * rank] = piece


def gram_part(state, part, rank):
    mine = state.pieces[part, :]
    first = dot(mine[:, : 2 * rank], state.pair[...])
    outer = jnp.concatenate([mine[:, :rank], mine[:, 2 * rank :]], axis=1)
    return halves(first) + dot(outer, state.single[...])


def conjugate_steps(state, base, rows_ref, scaled, hot, hot_t):
    groups, rank = state.x.shape
    for first in range(0, groups, state.block):
        part = pl.ds(first, state.block)
        r = halves(dot(hot_t[part, :], state.terms[...])) - gram_part(state, part, rank)
        if base is not None:
            r = r + base[part, :]
        state.r[part, :] = r
        state.p[part, :] = r
        squares = jnp.sum(r * r, axis=1, keepdims=True)
        state.squares[part, :] = jnp.broadcast_to(squares, r.shape)
    keep_pieces(state, slice(None), state.p[...])

    def step(last):
        pick_terms(state, rows_ref, scaled, None, hot)
        for first in range(0, groups, state.block):
            part = pl.ds(first, state.block)
            image = halves(dot(hot_t[part, :], state.terms[...])) + gram_part(state, part, rank)
            p = state.p[part, :]
            squares = state.squares[part, :]
            alpha = squares / jnp.sum(p * image, axis=1, keepdims=True)
            x = state.x[part, :] + alpha * p
            state.x[part, :] = x
            if last:
                keep_pieces(state, part, x)
                continue
            r = state.r[part, :] - alpha * image
            state.r[part, :] = r
            fresh = jnp.sum(r * r, axis=1, keepdims=True)
            p = r + (fresh / squares) * p
            state.p[part, :] = p
            state.squares[part, :] = jnp.broadcast_to(fresh, p.shape)
            keep_pieces(state, part, p)

    def middle(iteration, carry):
        step(False)
        return carry

    lax.fori_loop(0, ITERS - 1, middle, 0)
    step(True)


def body(
    n,
    fast,
    capacity,
    user_in,
    item_in,
    rhs_in,
    user_gram_in,
    count_in,
    asked_in,
    members_in,
    weight_in,
    rating_in,
    user_out,
    item_out,
    item_v,
    rhs_v,
    user_gram,
    count_v,
    asked_v,
    members_v,
    weight_v,
    rating_v,
    note_src,
    gathered,
    relay,
    notes,
    partial,
    near,
    across,
    whole,
    partial2,
    near2,
    across2,
    whole2,
    found,
    fetched,
    outgoing,
    arrived,
    user_scaled,
    user_coefs,
    item_scaled,
    item_coefs,
    user_hot,
    user_hot_t,
    item_hot,
    item_hot_t,
    pair,
    single,
    terms,
    user_r,
    user_p,
    user_squares,
    user_pieces,
    item_r,
    item_p,
    item_squares,
    item_pieces,
    send_sem,
    recv_sem,
    own_sem,
    load_sem,
):
    me = lax.axis_index("users") * fast + lax.axis_index("items")
    slots = n * capacity
    users, rank = user_out.shape
    items = item_out.shape[0]
    inner = near.shape[0]
    outer = across.shape[0]
    band = rank // inner
    seat, team = lax.rem(me, inner), lax.div(me, inner)
    region = CHUNK // capacity
    barrier = pltpu.get_barrier_semaphore()

    loads = [
        pltpu.make_async_copy(source, target, load_sem.at[index])
        for index, (source, target) in enumerate(
            (
                (count_in, count_v),
                (asked_in, asked_v),
                (members_in, members_v),
                (weight_in, weight_v),
                (rating_in, rating_v),
                (item_in, item_v),
                (user_in, user_out),
                (rhs_in, rhs_v),
                (user_gram_in, user_gram),
                (item_in, item_out),
            )
        )
    ]
    for load in loads:
        load.start()

    def at(peer):
        return (lax.div(peer, fast), lax.rem(peer, fast))

    def mate(step):
        return team * inner + lax.rem(seat + step, inner)

    def counterpart(step):
        return lax.rem(team + step, outer) * inner + seat

    for count, other in ((inner, mate), (outer, counterpart)):

        @pl.loop(1, count)
        def _(step):
            pl.semaphore_signal(barrier, inc=1, device_id=at(other(step)), device_id_type=MESH)

    def push(which, source, target, peer):
        pltpu.make_async_remote_copy(
            src_ref=source,
            dst_ref=target,
            send_sem=send_sem.at[which],
            recv_sem=recv_sem.at[which],
            device_id=at(peer),
            device_id_type=MESH,
        ).start()

    def landed(which, target):
        span = target.at[pl.ds(0, target.shape[0] - 1)]
        pltpu.make_async_copy(span, span, recv_sem.at[which]).wait()

    def sent(which, target):
        span = target.at[pl.ds(0, target.shape[0] - 1)]
        pltpu.make_async_copy(span, span, send_sem.at[which]).wait()

    def own(which, source, target):
        return pltpu.make_async_copy(source.at[me], target.at[me], own_sem.at[which])

    def gram_near(which, source, first):
        first[seat] = source[pl.ds(pl.multiple_of(seat * band, band), band), :]

        @pl.loop(1, inner)
        def _(step):
            other = lax.rem(seat + step, inner)
            push(
                which,
                source.at[pl.ds(pl.multiple_of(other * band, band), band)],
                first.at[seat],
                team * inner + other,
            )

    def gram_across(which, first, second):
        landed(which, first)
        second[team] = jnp.sum(first[...], axis=0)

        @pl.loop(1, outer)
        def _(step):
            other = lax.rem(team + step, outer)
            push(which + 1, second.at[team], second.at[team], other * inner + seat)

    def gram_back(which, second, third):
        landed(which + 1, second)
        third[seat] = jnp.sum(second[...], axis=0)

        @pl.loop(1, inner)
        def _(step):
            other = lax.rem(seat + step, inner)
            push(which + 2, third.at[seat], third.at[seat], team * inner + other)

    def gram_value(which, third):
        landed(which + 2, third)
        return third[...].reshape(rank, rank)

    def send_region(which, source, target, base):
        @pl.loop(0, region)
        def _(step):
            peer = base + lax.rem(me + step, region)

            @pl.when(peer != me)
            def _():
                push(which, source.at[peer], target.at[me], peer)

    def turn(step):
        return lax.rem(lax.axis_index("items") + step, slots // CHUNK)

    for load in loads[:5]:
        load.wait()
    live = iota((capacity, n), 0) < count_v[...]
    weights = jnp.where(live, weight_v[...], 0.0)
    coefs = jnp.where(live, (1.0 + weight_v[...]) * rating_v[...], 0.0)
    asked = asked_v[...].astype(F32)
    members = members_v[...].astype(F32)
    rest = jnp.zeros((rank - 4 * capacity, n), F32)
    own_note = jnp.concatenate([asked, weights, coefs, members, rest], axis=0).T
    for index in range(outer):
        note_src[:, index, :] = own_note[index * inner : (index + 1) * inner]
    pl.semaphore_wait(barrier, inner + outer - 2)

    @pl.loop(1, inner)
    def _(step):
        other = lax.rem(seat + step, inner)
        push(0, note_src.at[other], gathered.at[seat], mate(step))

    gathered[seat] = note_src[seat]
    loads[5].wait()
    mine = item_v[...]
    partial[...] = jnp.dot(
        mine.T, mine, precision=lax.Precision.HIGHEST, preferred_element_type=F32
    )
    landed(0, gathered)
    for index in range(outer):
        relay[index] = gathered[:, index, :]

    @pl.loop(1, outer)
    def _(step):
        other = lax.rem(team + step, outer)
        push(9, relay.at[other], notes.at[team], counterpart(step))

    notes[team] = relay[team]
    gram_near(3, partial, near)
    user_state = State(
        user_out, user_r, user_p, user_squares, user_pieces, terms, pair, single, users // 2
    )
    item_state = State(
        item_out, item_r, item_p, item_squares, item_pieces, terms, pair, single, items // 2
    )
    keep_pieces(item_state, slice(None), item_v[...])

    landed(9, notes)
    gram_across(3, near, across)
    all_notes = notes[...].reshape(n, rank)
    pieces = split3(all_notes)
    for step in range(slots // CHUNK):
        base = pl.multiple_of(turn(step) * region, region)
        wide = spread(pieces[:2], base, CHUNK, capacity, n)
        hot = column_table(wide, 0, capacity, items)
        item_hot[pl.ds(pl.multiple_of(base * capacity, CHUNK), CHUNK), :] = hot
        picked = halves(dot(hot, item_pieces[:, : 2 * rank]))
        picked = picked + dot(hot, item_pieces[:, 2 * rank :])
        found[pl.ds(base, region)] = picked.reshape(region, capacity, rank)
        if step == 1:
            gram_back(3, across, whole)
        send_region(1, found, fetched, base)
    own(1, found, fetched).start()

    own_pieces = split3(own_note)
    for first in range(0, slots, CHUNK):
        part = pl.ds(first, CHUNK)
        wide = spread(own_pieces, first // capacity, CHUNK, capacity, n)
        user_scaled[part, :] = jnp.broadcast_to(column(wide, 1, capacity), (CHUNK, rank))
        user_coefs[part, :] = jnp.broadcast_to(column(wide, 2, capacity), (CHUNK, rank))
        user_hot[part, :] = column_table(wide, 3, capacity, users)
    row_table(members, users, capacity, user_hot_t)
    loads[6].wait()
    set_gram(gram_value(3, whole), pair, single)
    for first in range(0, slots, CHUNK):
        part = pl.ds(first, CHUNK)
        wide = spread(pieces, first // capacity, CHUNK, capacity, n)
        item_scaled[part, :] = jnp.broadcast_to(column(wide, 1, capacity), (CHUNK, rank))
        item_coefs[part, :] = jnp.broadcast_to(column(wide, 2, capacity), (CHUNK, rank))
    row_table(all_notes.T[:capacity], items, capacity, item_hot_t)

    keep_pieces(user_state, slice(None), user_out[...])
    own(1, found, fetched).wait()
    landed(1, fetched)
    pick_terms(user_state, fetched, user_scaled, user_coefs, user_hot)
    conjugate_steps(user_state, None, fetched, user_scaled, user_hot, user_hot_t)

    refreshed = user_out[...]
    partial2[...] = jnp.dot(
        refreshed.T, refreshed, precision=lax.Precision.HIGHEST, preferred_element_type=F32
    )
    gram_near(6, partial2, near2)
    for step in range(slots // CHUNK):
        base = pl.multiple_of(turn(step) * region, region)
        hot = user_hot[pl.ds(pl.multiple_of(base * capacity, CHUNK), CHUNK), :]
        picked = halves(dot(hot, user_pieces[:, : 2 * rank]))
        picked = picked + dot(hot, user_pieces[:, 2 * rank :])
        outgoing[pl.ds(base, region)] = picked.reshape(region, capacity, rank)
        if step == 1:
            gram_across(6, near2, across2)
        send_region(2, outgoing, arrived, base)
    own(2, outgoing, arrived).start()
    gram_back(6, across2, whole2)

    for load in loads[7:]:
        load.wait()
    own(2, outgoing, arrived).wait()
    landed(2, arrived)
    pick_terms(item_state, arrived, item_scaled, item_coefs, item_hot)
    set_gram(user_gram[...] + gram_value(6, whole2), pair, single)
    conjugate_steps(item_state, rhs_v, arrived, item_scaled, item_hot, item_hot_t)
    for which, target in enumerate(
        (gathered, fetched, arrived, near, across, whole, near2, across2, whole2, notes)
    ):
        sent(which, target)


def per_device(
    user_old, item_old, item_rhs, user_gram, req_count, req_item, req_user, weight, rating
):
    fast = lax.axis_size("items")
    n = lax.axis_size("users") * fast
    capacity = req_item.shape[2]
    users, rank = user_old.shape
    items = item_old.shape[0]
    slots = n * capacity
    inner = 2 * fast
    outer = n // inner
    vmem = pl.BlockSpec(memory_space=pltpu.VMEM)
    hbm = pl.BlockSpec(memory_space=pltpu.HBM)

    def floats(*shape):
        return pltpu.VMEM(shape, F32)

    gram = [
        floats(rank, rank),
        floats(inner, rank // inner, rank),
        floats(outer, rank // inner, rank),
        floats(inner, rank // inner, rank),
    ]
    flip = lambda array: jnp.swapaxes(array[0], 0, 1)
    return pl.pallas_call(
        functools.partial(body, n, fast, capacity),
        out_shape=(
            jax.ShapeDtypeStruct((users, rank), F32),
            jax.ShapeDtypeStruct((items, rank), F32),
        ),
        in_specs=[hbm] * 9,
        out_specs=(vmem, vmem),
        scratch_shapes=[
            floats(items, rank),
            floats(items, rank),
            floats(rank, rank),
            pltpu.VMEM((1, n), jnp.int32),
            pltpu.VMEM((capacity, n), jnp.int32),
            pltpu.VMEM((capacity, n), jnp.int32),
            floats(capacity, n),
            floats(capacity, n),
            floats(inner, outer, rank),
            floats(inner, outer, rank),
            floats(outer, inner, rank),
            floats(outer, inner, rank),
            *gram,
            *gram,
            *[floats(n, capacity, rank)] * 4,
            *[floats(slots, rank)] * 4,
            pltpu.VMEM((slots, users), BF16),
            pltpu.VMEM((users, slots), BF16),
            pltpu.VMEM((slots, items), BF16),
            pltpu.VMEM((items, slots), BF16),
            pltpu.VMEM((2 * rank, 2 * rank), BF16),
            pltpu.VMEM((2 * rank, rank), BF16),
            pltpu.VMEM((slots, 2 * rank), BF16),
            *[floats(users, rank)] * 3,
            pltpu.VMEM((users, 3 * rank), BF16),
            *[floats(items, rank)] * 3,
            pltpu.VMEM((items, 3 * rank), BF16),
            pltpu.SemaphoreType.DMA((10,)),
            pltpu.SemaphoreType.DMA((10,)),
            pltpu.SemaphoreType.DMA((3,)),
            pltpu.SemaphoreType.DMA((10,)),
        ],
        compiler_params=pltpu.CompilerParams(
            collective_id=0, has_side_effects=True, vmem_limit_bytes=60 * 2**20
        ),
    )(
        user_old,
        item_old,
        item_rhs,
        user_gram,
        req_count,
        flip(req_item),
        flip(req_user),
        flip(weight),
        flip(rating),
    )


def solution(mesh):
    in_specs = (
        P(("users", "items"), None),
        P(("users", "items"), None),
        P(("users", "items"), None),
        P(),
        P(("users", "items"), None),
        P(("users", "items"), None, None),
        P(("users", "items"), None, None),
        P(("users", "items"), None, None),
        P(("users", "items"), None, None),
    )
    out_specs = (P(("users", "items"), None), P(("users", "items"), None))
    return jax.shard_map(
        per_device, mesh=mesh, in_specs=in_specs, out_specs=out_specs, check_vma=False
    )
```

```python
import functools
from typing import Any, NamedTuple
import jax
import jax.numpy as jnp
from jax import lax
from jax.sharding import PartitionSpec as P
from jax.experimental import pallas as pl
from jax.experimental.pallas import tpu as pltpu

ITERS = 8
RIDGE = 1.0
CHUNK = 512
PICK = 128
MESH = pl.DeviceIdType.MESH
F32 = jnp.float32
BF16 = jnp.bfloat16


def split2(value):
    high = value.astype(BF16)
    return high, (value - high.astype(F32)).astype(BF16)


def split3(value):
    high = value.astype(BF16)
    rest = value - high.astype(F32)
    middle = rest.astype(BF16)
    return high, middle, (rest - middle.astype(F32)).astype(BF16)


def dot(left, right):
    return jnp.dot(left, right, preferred_element_type=F32)


def halves(value):
    width = value.shape[1] // 2
    return value[:, :width] + value[:, width:]


def iota(shape, axis):
    return lax.broadcasted_iota(jnp.int32, shape, axis)


def owner_table(first, rows, capacity, senders):
    owner = lax.div(iota((rows, senders), 0), capacity) + first
    return (owner == iota((rows, senders), 1)).astype(F32).astype(BF16)


def spread(pieces, first, rows, capacity, senders):
    table = owner_table(first, rows, capacity, senders)
    wide = halves(dot(table, jnp.concatenate(pieces[:2], axis=1)))
    if len(pieces) > 2:
        wide = wide + dot(table, pieces[2])
    return wide


def column(wide, which, capacity):
    slot = lax.rem(iota(wide.shape, 0), capacity) + which * capacity
    return jnp.sum(jnp.where(slot == iota(wide.shape, 1), wide, 0.0), axis=1, keepdims=True)


def row_table(indices, groups, capacity, out):
    senders = indices.shape[1]
    both = jnp.concatenate(split2(indices), axis=0)
    slots = senders * capacity
    for first in range(0, slots, CHUNK):
        owner = lax.div(iota((senders, CHUNK), 1), capacity) + first // capacity
        table = (owner == iota((senders, CHUNK), 0)).astype(F32).astype(BF16)
        wide = dot(both, table)
        wide = wide[:capacity] + wide[capacity:]
        mine = iota(wide.shape, 0) == lax.rem(iota(wide.shape, 1), capacity)
        row = jnp.sum(jnp.where(mine, wide, 0.0), axis=0, keepdims=True).astype(jnp.int32)
        hot = (row == iota((groups, CHUNK), 0)).astype(F32).astype(BF16)
        out[:, pl.ds(first, CHUNK)] = hot


def column_table(wide, which, capacity, groups):
    index = column(wide, which, capacity).astype(jnp.int32)
    return (index == iota((wide.shape[0], groups), 1)).astype(F32).astype(BF16)


def set_gram(gram, pair, single):
    rank = gram.shape[0]
    ridge = jnp.where(iota((rank, rank), 0) == iota((rank, rank), 1), RIDGE, 0.0)
    high, middle, low = split3(gram + ridge)
    pair[...] = jnp.concatenate(
        [jnp.concatenate([high, middle], axis=1), jnp.concatenate([middle, high], axis=1)], axis=0
    )
    single[...] = jnp.concatenate([low, high], axis=0)


class State(NamedTuple):
    x: Any
    r: Any
    p: Any
    squares: Any
    pieces: Any
    terms: Any
    pair: Any
    single: Any
    block: int


def pick_terms(state, rows_ref, scaled, coefs, hot):
    slots, rank = scaled.shape
    capacity = rows_ref.shape[1]
    for first in range(0, slots, PICK):
        part = pl.ds(first, PICK)
        rows = rows_ref[pl.ds(first // capacity, PICK // capacity)].reshape(PICK, rank)
        picked = halves(dot(hot[part, :], state.pieces[:, : 2 * rank]))
        along = jnp.sum(rows * picked, axis=1, keepdims=True)
        if coefs is None:
            terms = along * scaled[part, :]
        else:
            weighted = scaled[part, :] * rows
            scaled[part, :] = weighted
            terms = coefs[part, :] * rows - along * weighted
        high, low = split2(terms)
        state.terms[part, :rank] = high
        state.terms[part, rank:] = low


def keep_pieces(state, part, value):
    rank = value.shape[1]
    for index, piece in enumerate(split3(value)):
        state.pieces[part, index * rank : (index + 1) * rank] = piece


def gram_part(state, part, rank):
    mine = state.pieces[part, :]
    first = dot(mine[:, : 2 * rank], state.pair[...])
    outer = jnp.concatenate([mine[:, :rank], mine[:, 2 * rank :]], axis=1)
    return halves(first) + dot(outer, state.single[...])


def fold_start(state, base, hot_t):
    groups = state.x.shape[0]
    for first in range(0, groups, state.block):
        part = pl.ds(first, state.block)
        r = halves(dot(hot_t[part, :], state.terms[...]))
        if base is not None:
            r = r + base[part, :]
        state.r[part, :] = r


def conjugate_steps(state, rows_ref, scaled, hot, hot_t):
    groups, rank = state.x.shape
    for first in range(0, groups, state.block):
        part = pl.ds(first, state.block)
        r = state.r[part, :] - gram_part(state, part, rank)
        state.r[part, :] = r
        state.p[part, :] = r
        squares = jnp.sum(r * r, axis=1, keepdims=True)
        state.squares[part, :] = jnp.broadcast_to(squares, r.shape)
        keep_pieces(state, part, r)

    def step(last):
        pick_terms(state, rows_ref, scaled, None, hot)
        for first in range(0, groups, state.block):
            part = pl.ds(first, state.block)
            image = halves(dot(hot_t[part, :], state.terms[...])) + gram_part(state, part, rank)
            p = state.p[part, :]
            squares = state.squares[part, :]
            alpha = squares / jnp.sum(p * image, axis=1, keepdims=True)
            x = state.x[part, :] + alpha * p
            state.x[part, :] = x
            if last:
                keep_pieces(state, part, x)
                continue
            r = state.r[part, :] - alpha * image
            state.r[part, :] = r
            fresh = jnp.sum(r * r, axis=1, keepdims=True)
            p = r + (fresh / squares) * p
            state.p[part, :] = p
            state.squares[part, :] = jnp.broadcast_to(fresh, p.shape)
            keep_pieces(state, part, p)

    def middle(iteration, carry):
        step(False)
        return carry

    lax.fori_loop(0, ITERS - 1, middle, 0)
    step(True)


def body(
    n,
    fast,
    capacity,
    user_in,
    item_in,
    rhs_in,
    user_gram_in,
    count_in,
    asked_in,
    members_in,
    weight_in,
    rating_in,
    user_out,
    item_out,
    user_x,
    item_x,
    item_v,
    rhs_v,
    user_gram,
    count_v,
    asked_v,
    members_v,
    weight_v,
    rating_v,
    note_src,
    gathered,
    relay,
    notes,
    whole,
    partial2,
    near2,
    across2,
    whole2,
    found,
    fetched,
    outgoing,
    arrived,
    user_scaled,
    user_coefs,
    item_scaled,
    item_coefs,
    user_hot,
    user_hot_t,
    item_hot,
    item_hot_t,
    pair,
    single,
    terms,
    user_r,
    user_p,
    user_squares,
    user_pieces,
    item_r,
    item_p,
    item_squares,
    item_pieces,
    send_sem,
    recv_sem,
    own_sem,
    load_sem,
):
    me = lax.axis_index("users") * fast + lax.axis_index("items")
    slots = n * capacity
    users, rank = user_out.shape
    items = item_out.shape[0]
    inner = near2.shape[0]
    outer = across2.shape[0]
    band = rank // inner
    seat, team = lax.rem(me, inner), lax.div(me, inner)
    region = CHUNK // capacity
    barrier = pltpu.get_barrier_semaphore()

    loads = [
        pltpu.make_async_copy(source, target, load_sem.at[index])
        for index, (source, target) in enumerate(
            (
                (count_in, count_v),
                (asked_in, asked_v),
                (members_in, members_v),
                (weight_in, weight_v),
                (rating_in, rating_v),
                (item_in, item_v),
                (user_in, user_x),
                (rhs_in, rhs_v),
                (user_gram_in, user_gram),
                (item_in, item_x),
            )
        )
    ]
    for load in loads:
        load.start()

    def at(peer):
        return (lax.div(peer, fast), lax.rem(peer, fast))

    def mate(step):
        return team * inner + lax.rem(seat + step, inner)

    def counterpart(step):
        return lax.rem(team + step, outer) * inner + seat

    for count, other in ((inner, mate), (outer, counterpart)):

        @pl.loop(1, count)
        def _(step):
            pl.semaphore_signal(barrier, inc=1, device_id=at(other(step)), device_id_type=MESH)

    def push(which, source, target, peer):
        pltpu.make_async_remote_copy(
            src_ref=source,
            dst_ref=target,
            send_sem=send_sem.at[which],
            recv_sem=recv_sem.at[which],
            device_id=at(peer),
            device_id_type=MESH,
        ).start()

    def landed(which, target):
        span = target.at[pl.ds(0, target.shape[0] - 1)]
        pltpu.make_async_copy(span, span, recv_sem.at[which]).wait()

    def sent(which, target):
        span = target.at[pl.ds(0, target.shape[0] - 1)]
        pltpu.make_async_copy(span, span, send_sem.at[which]).wait()

    def own(which, source, target):
        return pltpu.make_async_copy(source.at[me], target.at[me], own_sem.at[which])

    def gram_near(which, source, first):
        first[seat] = source[pl.ds(pl.multiple_of(seat * band, band), band), :]

        @pl.loop(1, inner)
        def _(step):
            other = lax.rem(seat + step, inner)
            push(
                which,
                source.at[pl.ds(pl.multiple_of(other * band, band), band)],
                first.at[seat],
                team * inner + other,
            )

    def gram_across(which, first, second):
        landed(which, first)
        second[team] = jnp.sum(first[...], axis=0)

        @pl.loop(1, outer)
        def _(step):
            other = lax.rem(team + step, outer)
            push(which + 1, second.at[team], second.at[team], other * inner + seat)

    def give_back(which, third):
        @pl.loop(1, inner)
        def _(step):
            other = lax.rem(seat + step, inner)
            push(which, third.at[seat], third.at[seat], team * inner + other)

    def gram_back(which, second, third):
        landed(which + 1, second)
        third[seat] = jnp.sum(second[...], axis=0)
        give_back(which + 2, third)

    def send_region(which, source, target, base):
        @pl.loop(0, region)
        def _(step):
            peer = base + lax.rem(me + step, region)

            @pl.when(peer != me)
            def _():
                push(which, source.at[peer], target.at[me], peer)

    def turn(step):
        return lax.rem(lax.axis_index("items") + step, slots // CHUNK)

    for load in loads[:5]:
        load.wait()
    live = iota((capacity, n), 0) < count_v[...]
    weights = jnp.where(live, weight_v[...], 0.0)
    coefs = jnp.where(live, (1.0 + weight_v[...]) * rating_v[...], 0.0)
    asked = asked_v[...].astype(F32)
    members = members_v[...].astype(F32)
    rest = jnp.zeros((rank - 4 * capacity, n), F32)
    own_note = jnp.concatenate([asked, weights, coefs, members, rest], axis=0).T
    for index in range(outer):
        note_src[:, index, :] = own_note[index * inner : (index + 1) * inner]
    loads[5].wait()
    mine = item_v[...]
    gram = jnp.dot(mine.T, mine, precision=lax.Precision.HIGHEST, preferred_element_type=F32)
    note_src[:, outer:, :] = gram.reshape(inner, band, rank)
    pl.semaphore_wait(barrier, inner + outer - 2)

    @pl.loop(1, inner)
    def _(step):
        other = lax.rem(seat + step, inner)
        push(0, note_src.at[other], gathered.at[seat], mate(step))

    gathered[seat] = note_src[seat]
    landed(0, gathered)
    for index in range(outer):
        relay[index, :inner] = gathered[:, index, :]
    team_sum = jnp.sum(gathered[:, outer:, :], axis=0)
    relay[:, inner:, :] = jnp.broadcast_to(team_sum[None], (outer, band, rank))

    @pl.loop(1, outer)
    def _(step):
        other = lax.rem(team + step, outer)
        push(6, relay.at[other], notes.at[team], counterpart(step))

    notes[team] = relay[team]
    user_state = State(
        user_x, user_r, user_p, user_squares, user_pieces, terms, pair, single, users // 2
    )
    item_state = State(
        item_x, item_r, item_p, item_squares, item_pieces, terms, pair, single, items // 2
    )
    keep_pieces(item_state, slice(None), item_v[...])

    landed(6, notes)
    whole[seat] = jnp.sum(notes[:, inner:, :], axis=0)
    give_back(7, whole)
    all_notes = notes[:, :inner, :].reshape(n, rank)
    pieces = split3(all_notes)
    for step in range(slots // CHUNK):
        base = pl.multiple_of(turn(step) * region, region)
        wide = spread(pieces[:2], base, CHUNK, capacity, n)
        hot = column_table(wide, 0, capacity, items)
        item_hot[pl.ds(pl.multiple_of(base * capacity, CHUNK), CHUNK), :] = hot
        picked = halves(dot(hot, item_pieces[:, : 2 * rank]))
        picked = picked + dot(hot, item_pieces[:, 2 * rank :])
        found[pl.ds(base, region)] = picked.reshape(region, capacity, rank)
        send_region(1, found, fetched, base)
    own(1, found, fetched).start()

    own_pieces = split3(own_note)
    for first in range(0, slots, CHUNK):
        part = pl.ds(first, CHUNK)
        wide = spread(own_pieces, first // capacity, CHUNK, capacity, n)
        user_scaled[part, :] = jnp.broadcast_to(column(wide, 1, capacity), (CHUNK, rank))
        user_coefs[part, :] = jnp.broadcast_to(column(wide, 2, capacity), (CHUNK, rank))
        user_hot[part, :] = column_table(wide, 3, capacity, users)
    row_table(members, users, capacity, user_hot_t)
    loads[6].wait()
    for first in range(0, slots, CHUNK):
        part = pl.ds(first, CHUNK)
        wide = spread(pieces, first // capacity, CHUNK, capacity, n)
        item_scaled[part, :] = jnp.broadcast_to(column(wide, 1, capacity), (CHUNK, rank))
        item_coefs[part, :] = jnp.broadcast_to(column(wide, 2, capacity), (CHUNK, rank))
    row_table(all_notes.T[:capacity], items, capacity, item_hot_t)

    keep_pieces(user_state, slice(None), user_x[...])
    own(1, found, fetched).wait()
    landed(1, fetched)
    pick_terms(user_state, fetched, user_scaled, user_coefs, user_hot)
    fold_start(user_state, None, user_hot_t)
    landed(7, whole)
    set_gram(whole[...].reshape(rank, rank), pair, single)
    conjugate_steps(user_state, fetched, user_scaled, user_hot, user_hot_t)
    put = pltpu.make_async_copy(user_x, user_out, load_sem.at[10])
    put.start()

    refreshed = user_x[...]
    partial2[...] = jnp.dot(
        refreshed.T, refreshed, precision=lax.Precision.HIGHEST, preferred_element_type=F32
    )
    gram_near(3, partial2, near2)
    for step in range(slots // CHUNK):
        base = pl.multiple_of(turn(step) * region, region)
        hot = user_hot[pl.ds(pl.multiple_of(base * capacity, CHUNK), CHUNK), :]
        picked = halves(dot(hot, user_pieces[:, : 2 * rank]))
        picked = picked + dot(hot, user_pieces[:, 2 * rank :])
        outgoing[pl.ds(base, region)] = picked.reshape(region, capacity, rank)
        if step == 1:
            gram_across(3, near2, across2)
        send_region(2, outgoing, arrived, base)
    own(2, outgoing, arrived).start()
    gram_back(3, across2, whole2)

    for load in loads[7:]:
        load.wait()
    own(2, outgoing, arrived).wait()
    landed(2, arrived)
    pick_terms(item_state, arrived, item_scaled, item_coefs, item_hot)
    fold_start(item_state, rhs_v, item_hot_t)
    landed(5, whole2)
    set_gram(user_gram[...] + whole2[...].reshape(rank, rank), pair, single)
    conjugate_steps(item_state, arrived, item_scaled, item_hot, item_hot_t)
    final = pltpu.make_async_copy(item_x, item_out, load_sem.at[11])
    final.start()
    put.wait()
    for which, target in enumerate(
        (gathered, fetched, arrived, near2, across2, whole2, notes, whole)
    ):
        sent(which, target)
    final.wait()


def hand_on(user_in, item_in, user_out, item_out, user_v, item_v, sems):
    steps = []
    half = item_in.shape[0] // 2
    for source, middle, target, part in (
        (item_in, item_v, item_out, pl.ds(0, half)),
        (item_in, item_v, item_out, pl.ds(half, half)),
        (user_in, user_v, user_out, pl.ds(0, user_in.shape[0])),
    ):
        index = len(steps)
        steps.append(
            (
                pltpu.make_async_copy(source.at[part], middle.at[part], sems.at[0, index]),
                pltpu.make_async_copy(middle.at[part], target.at[part], sems.at[1, index]),
            )
        )
    for first, _ in steps:
        first.start()
    for first, second in steps:
        first.wait()
        second.start()
    for _, second in steps:
        second.wait()


def per_device(
    user_old, item_old, item_rhs, user_gram, req_count, req_item, req_user, weight, rating
):
    fast = lax.axis_size("items")
    n = lax.axis_size("users") * fast
    capacity = req_item.shape[2]
    users, rank = user_old.shape
    items = item_old.shape[0]
    slots = n * capacity
    inner = 2 * fast
    outer = n // inner
    anywhere = pl.BlockSpec(memory_space=pl.ANY)

    def floats(*shape):
        return pltpu.VMEM(shape, F32)

    gram = [
        floats(rank, rank),
        floats(inner, rank // inner, rank),
        floats(outer, rank // inner, rank),
        floats(inner, rank // inner, rank),
    ]
    flip = lambda array: jnp.swapaxes(array[0], 0, 1)
    results = pl.pallas_call(
        functools.partial(body, n, fast, capacity),
        out_shape=(
            jax.ShapeDtypeStruct((users, rank), F32),
            jax.ShapeDtypeStruct((items, rank), F32),
        ),
        in_specs=[anywhere] * 9,
        out_specs=(anywhere, anywhere),
        scratch_shapes=[
            floats(users, rank),
            floats(items, rank),
            floats(items, rank),
            floats(items, rank),
            floats(rank, rank),
            pltpu.VMEM((1, n), jnp.int32),
            pltpu.VMEM((capacity, n), jnp.int32),
            pltpu.VMEM((capacity, n), jnp.int32),
            floats(capacity, n),
            floats(capacity, n),
            floats(inner, outer + rank // inner, rank),
            floats(inner, outer + rank // inner, rank),
            floats(outer, inner + rank // inner, rank),
            floats(outer, inner + rank // inner, rank),
            gram[3],
            *gram,
            *[floats(n, capacity, rank)] * 4,
            *[floats(slots, rank)] * 4,
            pltpu.VMEM((slots, users), BF16),
            pltpu.VMEM((users, slots), BF16),
            pltpu.VMEM((slots, items), BF16),
            pltpu.VMEM((items, slots), BF16),
            pltpu.VMEM((2 * rank, 2 * rank), BF16),
            pltpu.VMEM((2 * rank, rank), BF16),
            pltpu.VMEM((slots, 2 * rank), BF16),
            *[floats(users, rank)] * 3,
            pltpu.VMEM((users, 3 * rank), BF16),
            *[floats(items, rank)] * 3,
            pltpu.VMEM((items, 3 * rank), BF16),
            pltpu.SemaphoreType.DMA((8,)),
            pltpu.SemaphoreType.DMA((8,)),
            pltpu.SemaphoreType.DMA((3,)),
            pltpu.SemaphoreType.DMA((12,)),
        ],
        compiler_params=pltpu.CompilerParams(
            collective_id=0, has_side_effects=True, vmem_limit_bytes=60 * 2**20
        ),
    )(
        user_old,
        item_old,
        item_rhs,
        user_gram,
        req_count,
        flip(req_item),
        flip(req_user),
        flip(weight),
        flip(rating),
    )
    return pl.pallas_call(
        hand_on,
        out_shape=tuple(jax.ShapeDtypeStruct(array.shape, F32) for array in results),
        in_specs=[anywhere] * 2,
        out_specs=(anywhere, anywhere),
        scratch_shapes=[floats(users, rank), floats(items, rank), pltpu.SemaphoreType.DMA((2, 3))],
        compiler_params=pltpu.CompilerParams(vmem_limit_bytes=60 * 2**20),
    )(*results)


def solution(mesh):
    in_specs = (
        P(("users", "items"), None),
        P(("users", "items"), None),
        P(("users", "items"), None),
        P(),
        P(("users", "items"), None),
        P(("users", "items"), None, None),
        P(("users", "items"), None, None),
        P(("users", "items"), None, None),
        P(("users", "items"), None, None),
    )
    out_specs = (P(("users", "items"), None), P(("users", "items"), None))
    return jax.shard_map(
        per_device, mesh=mesh, in_specs=in_specs, out_specs=out_specs, check_vma=False
    )
```

```python
import functools
from typing import Any, NamedTuple
import jax
import jax.numpy as jnp
from jax import lax
from jax.sharding import PartitionSpec as P
from jax.experimental import pallas as pl
from jax.experimental.pallas import tpu as pltpu

ITERS = 8
RIDGE = 1.0
CHUNK = 512
PICK = 128
MESH = pl.DeviceIdType.MESH
F32 = jnp.float32
BF16 = jnp.bfloat16


def split2(value):
    high = value.astype(BF16)
    return high, (value - high.astype(F32)).astype(BF16)


def split3(value):
    high = value.astype(BF16)
    rest = value - high.astype(F32)
    middle = rest.astype(BF16)
    return high, middle, (rest - middle.astype(F32)).astype(BF16)


def dot(left, right):
    return jnp.dot(left, right, preferred_element_type=F32)


def halves(value):
    width = value.shape[1] // 2
    return value[:, :width] + value[:, width:]


def iota(shape, axis):
    return lax.broadcasted_iota(jnp.int32, shape, axis)


def owner_table(first, rows, capacity, senders):
    owner = lax.div(iota((rows, senders), 0), capacity) + first
    return (owner == iota((rows, senders), 1)).astype(F32).astype(BF16)


def spread(pieces, first, rows, capacity, senders):
    table = owner_table(first, rows, capacity, senders)
    wide = halves(dot(table, jnp.concatenate(pieces[:2], axis=1)))
    if len(pieces) > 2:
        wide = wide + dot(table, pieces[2])
    return wide


def column(wide, which, capacity):
    slot = lax.rem(iota(wide.shape, 0), capacity) + which * capacity
    return jnp.sum(jnp.where(slot == iota(wide.shape, 1), wide, 0.0), axis=1, keepdims=True)


def row_table(indices, groups, capacity, out):
    senders = indices.shape[1]
    both = jnp.concatenate(split2(indices), axis=0)
    slots = senders * capacity
    for first in range(0, slots, CHUNK):
        owner = lax.div(iota((senders, CHUNK), 1), capacity) + first // capacity
        table = (owner == iota((senders, CHUNK), 0)).astype(F32).astype(BF16)
        wide = dot(both, table)
        wide = wide[:capacity] + wide[capacity:]
        mine = iota(wide.shape, 0) == lax.rem(iota(wide.shape, 1), capacity)
        row = jnp.sum(jnp.where(mine, wide, 0.0), axis=0, keepdims=True).astype(jnp.int32)
        hot = (row == iota((groups, CHUNK), 0)).astype(F32).astype(BF16)
        out[:, pl.ds(first, CHUNK)] = hot


def column_table(wide, which, capacity, groups):
    index = column(wide, which, capacity).astype(jnp.int32)
    return (index == iota((wide.shape[0], groups), 1)).astype(F32).astype(BF16)


def set_gram(gram, pair, single):
    rank = gram.shape[0]
    ridge = jnp.where(iota((rank, rank), 0) == iota((rank, rank), 1), RIDGE, 0.0)
    high, middle, low = split3(gram + ridge)
    pair[...] = jnp.concatenate(
        [jnp.concatenate([high, middle], axis=1), jnp.concatenate([middle, high], axis=1)], axis=0
    )
    single[...] = jnp.concatenate([low, high], axis=0)


class State(NamedTuple):
    x: Any
    r: Any
    p: Any
    squares: Any
    pieces: Any
    terms: Any
    pair: Any
    single: Any
    block: int


def pick_terms(state, rows_ref, scaled, coefs, hot):
    slots, rank = scaled.shape
    capacity = rows_ref.shape[1]
    for first in range(0, slots, PICK):
        part = pl.ds(first, PICK)
        rows = rows_ref[pl.ds(first // capacity, PICK // capacity)].reshape(PICK, rank)
        picked = halves(dot(hot[part, :], state.pieces[:, : 2 * rank]))
        along = jnp.sum(rows * picked, axis=1, keepdims=True)
        if coefs is None:
            terms = along * scaled[part, :]
        else:
            weighted = scaled[part, :] * rows
            scaled[part, :] = weighted
            terms = coefs[part, :] * rows - along * weighted
        high, low = split2(terms)
        state.terms[part, :rank] = high
        state.terms[part, rank:] = low


def keep_pieces(state, part, value):
    rank = value.shape[1]
    for index, piece in enumerate(split3(value)):
        state.pieces[part, index * rank : (index + 1) * rank] = piece


def gram_part(state, part, rank):
    mine = state.pieces[part, :]
    first = dot(mine[:, : 2 * rank], state.pair[...])
    outer = jnp.concatenate([mine[:, :rank], mine[:, 2 * rank :]], axis=1)
    return halves(first) + dot(outer, state.single[...])


def fold_start(state, base, hot_t):
    groups = state.x.shape[0]
    for first in range(0, groups, state.block):
        part = pl.ds(first, state.block)
        r = halves(dot(hot_t[part, :], state.terms[...]))
        if base is not None:
            r = r + base[part, :]
        state.r[part, :] = r


def conjugate_steps(state, rows_ref, scaled, hot, hot_t):
    groups, rank = state.x.shape
    for first in range(0, groups, state.block):
        part = pl.ds(first, state.block)
        r = state.r[part, :] - gram_part(state, part, rank)
        state.r[part, :] = r
        state.p[part, :] = r
        squares = jnp.sum(r * r, axis=1, keepdims=True)
        state.squares[part, :] = jnp.broadcast_to(squares, r.shape)
        keep_pieces(state, part, r)

    def step(last):
        pick_terms(state, rows_ref, scaled, None, hot)
        for first in range(0, groups, state.block):
            part = pl.ds(first, state.block)
            image = halves(dot(hot_t[part, :], state.terms[...])) + gram_part(state, part, rank)
            p = state.p[part, :]
            squares = state.squares[part, :]
            alpha = squares / jnp.sum(p * image, axis=1, keepdims=True)
            x = state.x[part, :] + alpha * p
            state.x[part, :] = x
            if last:
                keep_pieces(state, part, x)
                continue
            r = state.r[part, :] - alpha * image
            state.r[part, :] = r
            fresh = jnp.sum(r * r, axis=1, keepdims=True)
            p = r + (fresh / squares) * p
            state.p[part, :] = p
            state.squares[part, :] = jnp.broadcast_to(fresh, p.shape)
            keep_pieces(state, part, p)

    def middle(iteration, carry):
        step(False)
        return carry

    lax.fori_loop(0, ITERS - 1, middle, 0)
    step(True)


def body(
    n,
    fast,
    capacity,
    user_in,
    item_in,
    rhs_in,
    user_gram_in,
    count_in,
    asked_in,
    members_in,
    weight_in,
    rating_in,
    user_out,
    item_out,
    item_v,
    rhs_v,
    user_gram,
    count_v,
    asked_v,
    members_v,
    weight_v,
    rating_v,
    note_src,
    gathered,
    relay,
    notes,
    partial,
    near,
    across,
    whole,
    partial2,
    near2,
    across2,
    whole2,
    found,
    fetched,
    outgoing,
    arrived,
    user_scaled,
    user_coefs,
    item_scaled,
    item_coefs,
    user_hot,
    user_hot_t,
    item_hot,
    item_hot_t,
    pair,
    single,
    terms,
    user_r,
    user_p,
    user_squares,
    user_pieces,
    item_r,
    item_p,
    item_squares,
    item_pieces,
    send_sem,
    recv_sem,
    own_sem,
    load_sem,
):
    me = lax.axis_index("users") * fast + lax.axis_index("items")
    slots = n * capacity
    users, rank = user_out.shape
    items = item_out.shape[0]
    inner = near2.shape[0]
    outer = across2.shape[0]
    band = rank // inner
    seat, team = lax.rem(me, inner), lax.div(me, inner)
    region = CHUNK // capacity
    barrier = pltpu.get_barrier_semaphore()

    loads = [
        pltpu.make_async_copy(source, target, load_sem.at[index])
        for index, (source, target) in enumerate(
            (
                (count_in, count_v),
                (asked_in, asked_v),
                (members_in, members_v),
                (weight_in, weight_v),
                (rating_in, rating_v),
                (item_in, item_v),
                (user_in, user_out),
                (rhs_in, rhs_v),
                (user_gram_in, user_gram),
                (item_in, item_out),
            )
        )
    ]
    for load in loads:
        load.start()

    def at(peer):
        return (lax.div(peer, fast), lax.rem(peer, fast))

    def mate(step):
        return team * inner + lax.rem(seat + step, inner)

    def counterpart(step):
        return lax.rem(team + step, outer) * inner + seat

    for count, other in ((inner, mate), (outer, counterpart)):

        @pl.loop(1, count)
        def _(step):
            pl.semaphore_signal(barrier, inc=1, device_id=at(other(step)), device_id_type=MESH)

    def push(which, source, target, peer):
        pltpu.make_async_remote_copy(
            src_ref=source,
            dst_ref=target,
            send_sem=send_sem.at[which],
            recv_sem=recv_sem.at[which],
            device_id=at(peer),
            device_id_type=MESH,
        ).start()

    def landed(which, target):
        span = target.at[pl.ds(0, target.shape[0] - 1)]
        pltpu.make_async_copy(span, span, recv_sem.at[which]).wait()

    def sent(which, target):
        span = target.at[pl.ds(0, target.shape[0] - 1)]
        pltpu.make_async_copy(span, span, send_sem.at[which]).wait()

    def own(which, source, target):
        return pltpu.make_async_copy(source.at[me], target.at[me], own_sem.at[which])

    def gram_near(which, source, first):
        first[seat] = source[pl.ds(pl.multiple_of(seat * band, band), band), :]

        @pl.loop(1, inner)
        def _(step):
            other = lax.rem(seat + step, inner)
            push(
                which,
                source.at[pl.ds(pl.multiple_of(other * band, band), band)],
                first.at[seat],
                team * inner + other,
            )

    def gram_across(which, first, second):
        landed(which, first)
        second[team] = jnp.sum(first[...], axis=0)

        @pl.loop(1, outer)
        def _(step):
            other = lax.rem(team + step, outer)
            push(which + 1, second.at[team], second.at[team], other * inner + seat)

    def give_back(which, third):
        @pl.loop(1, inner)
        def _(step):
            other = lax.rem(seat + step, inner)
            push(which, third.at[seat], third.at[seat], team * inner + other)

    def gram_back(which, second, third):
        landed(which + 1, second)
        third[seat] = jnp.sum(second[...], axis=0)
        give_back(which + 2, third)

    def send_region(which, source, target, base):
        @pl.loop(0, region)
        def _(step):
            peer = base + lax.rem(me + step, region)

            @pl.when(peer != me)
            def _():
                push(which, source.at[peer], target.at[me], peer)

    def turn(step):
        return lax.rem(lax.axis_index("items") + step, slots // CHUNK)

    for load in loads[:5]:
        load.wait()
    live = iota((capacity, n), 0) < count_v[...]
    weights = jnp.where(live, weight_v[...], 0.0)
    coefs = jnp.where(live, (1.0 + weight_v[...]) * rating_v[...], 0.0)
    asked = asked_v[...].astype(F32)
    members = members_v[...].astype(F32)
    rest = jnp.zeros((rank - 4 * capacity, n), F32)
    own_note = jnp.concatenate([asked, weights, coefs, members, rest], axis=0).T
    for index in range(outer):
        note_src[:, index, :] = own_note[index * inner : (index + 1) * inner]
    pl.semaphore_wait(barrier, inner + outer - 2)

    @pl.loop(1, inner)
    def _(step):
        other = lax.rem(seat + step, inner)
        push(0, note_src.at[other], gathered.at[seat], mate(step))

    gathered[seat] = note_src[seat]
    loads[5].wait()
    mine = item_v[...]
    partial[...] = jnp.dot(
        mine.T, mine, precision=lax.Precision.HIGHEST, preferred_element_type=F32
    )
    gram_near(7, partial, near)
    landed(0, gathered)
    for index in range(outer):
        relay[index] = gathered[:, index, :]

    @pl.loop(1, outer)
    def _(step):
        other = lax.rem(team + step, outer)
        push(6, relay.at[other], notes.at[team], counterpart(step))

    notes[team] = relay[team]
    landed(7, near)
    across[team] = jnp.sum(near[...], axis=0)

    @pl.loop(1, outer)
    def _(step):
        push(8, across.at[team], across.at[team], counterpart(step))

    user_state = State(
        user_out, user_r, user_p, user_squares, user_pieces, terms, pair, single, users // 2
    )
    item_state = State(
        item_out, item_r, item_p, item_squares, item_pieces, terms, pair, single, items // 2
    )
    keep_pieces(item_state, slice(None), item_v[...])

    landed(6, notes)
    all_notes = notes[...].reshape(n, rank)
    pieces = split3(all_notes)
    for step in range(slots // CHUNK):
        base = pl.multiple_of(turn(step) * region, region)
        wide = spread(pieces[:2], base, CHUNK, capacity, n)
        hot = column_table(wide, 0, capacity, items)
        item_hot[pl.ds(pl.multiple_of(base * capacity, CHUNK), CHUNK), :] = hot
        picked = halves(dot(hot, item_pieces[:, : 2 * rank]))
        picked = picked + dot(hot, item_pieces[:, 2 * rank :])
        found[pl.ds(base, region)] = picked.reshape(region, capacity, rank)
        send_region(1, found, fetched, base)
        if step == 0:
            landed(8, across)
            whole[seat] = jnp.sum(across[...], axis=0)
            give_back(9, whole)
    own(1, found, fetched).start()

    own_pieces = split3(own_note)
    for first in range(0, slots, CHUNK):
        part = pl.ds(first, CHUNK)
        wide = spread(own_pieces, first // capacity, CHUNK, capacity, n)
        user_scaled[part, :] = jnp.broadcast_to(column(wide, 1, capacity), (CHUNK, rank))
        user_coefs[part, :] = jnp.broadcast_to(column(wide, 2, capacity), (CHUNK, rank))
        user_hot[part, :] = column_table(wide, 3, capacity, users)
    row_table(members, users, capacity, user_hot_t)
    loads[6].wait()
    for first in range(0, slots, CHUNK):
        part = pl.ds(first, CHUNK)
        wide = spread(pieces, first // capacity, CHUNK, capacity, n)
        item_scaled[part, :] = jnp.broadcast_to(column(wide, 1, capacity), (CHUNK, rank))
        item_coefs[part, :] = jnp.broadcast_to(column(wide, 2, capacity), (CHUNK, rank))
    row_table(all_notes.T[:capacity], items, capacity, item_hot_t)

    keep_pieces(user_state, slice(None), user_out[...])
    own(1, found, fetched).wait()
    landed(1, fetched)
    pick_terms(user_state, fetched, user_scaled, user_coefs, user_hot)
    fold_start(user_state, None, user_hot_t)
    landed(9, whole)
    set_gram(whole[...].reshape(rank, rank), pair, single)
    conjugate_steps(user_state, fetched, user_scaled, user_hot, user_hot_t)

    refreshed = user_out[...]
    partial2[...] = jnp.dot(
        refreshed.T, refreshed, precision=lax.Precision.HIGHEST, preferred_element_type=F32
    )
    gram_near(3, partial2, near2)
    for step in range(slots // CHUNK):
        base = pl.multiple_of(turn(step) * region, region)
        hot = user_hot[pl.ds(pl.multiple_of(base * capacity, CHUNK), CHUNK), :]
        picked = halves(dot(hot, user_pieces[:, : 2 * rank]))
        picked = picked + dot(hot, user_pieces[:, 2 * rank :])
        outgoing[pl.ds(base, region)] = picked.reshape(region, capacity, rank)
        if step == 1:
            gram_across(3, near2, across2)
        send_region(2, outgoing, arrived, base)
    own(2, outgoing, arrived).start()
    gram_back(3, across2, whole2)

    for load in loads[7:]:
        load.wait()
    own(2, outgoing, arrived).wait()
    landed(2, arrived)
    pick_terms(item_state, arrived, item_scaled, item_coefs, item_hot)
    fold_start(item_state, rhs_v, item_hot_t)
    landed(5, whole2)
    set_gram(user_gram[...] + whole2[...].reshape(rank, rank), pair, single)
    conjugate_steps(item_state, arrived, item_scaled, item_hot, item_hot_t)
    for which, target in enumerate(
        (gathered, fetched, arrived, near2, across2, whole2, notes, near, across, whole)
    ):
        sent(which, target)


def hand_on(user_in, item_in, user_out, item_out, sems):
    moves = [
        pltpu.make_async_copy(item_in, item_out, sems.at[0]),
        pltpu.make_async_copy(user_in, user_out, sems.at[1]),
    ]
    for move in moves:
        move.start()
    for move in moves:
        move.wait()


def per_device(
    user_old, item_old, item_rhs, user_gram, req_count, req_item, req_user, weight, rating
):
    fast = lax.axis_size("items")
    n = lax.axis_size("users") * fast
    capacity = req_item.shape[2]
    users, rank = user_old.shape
    items = item_old.shape[0]
    slots = n * capacity
    inner = 2 * fast
    outer = n // inner
    anywhere = pl.BlockSpec(memory_space=pl.ANY)
    vmem = pl.BlockSpec(memory_space=pltpu.VMEM)

    def floats(*shape):
        return pltpu.VMEM(shape, F32)

    gram = [
        floats(rank, rank),
        floats(inner, rank // inner, rank),
        floats(outer, rank // inner, rank),
        floats(inner, rank // inner, rank),
    ]
    flip = lambda array: jnp.swapaxes(array[0], 0, 1)
    results = pl.pallas_call(
        functools.partial(body, n, fast, capacity),
        out_shape=(floats(users, rank), floats(items, rank)),
        in_specs=[anywhere] * 9,
        out_specs=(vmem, vmem),
        scratch_shapes=[
            floats(items, rank),
            floats(items, rank),
            floats(rank, rank),
            pltpu.VMEM((1, n), jnp.int32),
            pltpu.VMEM((capacity, n), jnp.int32),
            pltpu.VMEM((capacity, n), jnp.int32),
            floats(capacity, n),
            floats(capacity, n),
            floats(inner, outer, rank),
            floats(inner, outer, rank),
            floats(outer, inner, rank),
            floats(outer, inner, rank),
            *gram,
            *gram,
            *[floats(n, capacity, rank)] * 4,
            *[floats(slots, rank)] * 4,
            pltpu.VMEM((slots, users), BF16),
            pltpu.VMEM((users, slots), BF16),
            pltpu.VMEM((slots, items), BF16),
            pltpu.VMEM((items, slots), BF16),
            pltpu.VMEM((2 * rank, 2 * rank), BF16),
            pltpu.VMEM((2 * rank, rank), BF16),
            pltpu.VMEM((slots, 2 * rank), BF16),
            *[floats(users, rank)] * 3,
            pltpu.VMEM((users, 3 * rank), BF16),
            *[floats(items, rank)] * 3,
            pltpu.VMEM((items, 3 * rank), BF16),
            pltpu.SemaphoreType.DMA((10,)),
            pltpu.SemaphoreType.DMA((10,)),
            pltpu.SemaphoreType.DMA((3,)),
            pltpu.SemaphoreType.DMA((10,)),
        ],
        compiler_params=pltpu.CompilerParams(
            collective_id=0, has_side_effects=True, vmem_limit_bytes=60 * 2**20
        ),
    )(
        user_old,
        item_old,
        item_rhs,
        user_gram,
        req_count,
        flip(req_item),
        flip(req_user),
        flip(weight),
        flip(rating),
    )
    return pl.pallas_call(
        hand_on,
        out_shape=tuple(jax.ShapeDtypeStruct(array.shape, F32) for array in results),
        in_specs=[vmem] * 2,
        out_specs=(anywhere, anywhere),
        scratch_shapes=[pltpu.SemaphoreType.DMA((2,))],
        compiler_params=pltpu.CompilerParams(vmem_limit_bytes=2 * 2**20),
    )(*results)


def solution(mesh):
    in_specs = (
        P(("users", "items"), None),
        P(("users", "items"), None),
        P(("users", "items"), None),
        P(),
        P(("users", "items"), None),
        P(("users", "items"), None, None),
        P(("users", "items"), None, None),
        P(("users", "items"), None, None),
        P(("users", "items"), None, None),
    )
    out_specs = (P(("users", "items"), None), P(("users", "items"), None))
    return jax.shard_map(
        per_device, mesh=mesh, in_specs=in_specs, out_specs=out_specs, check_vma=False
    )
```

```python
import functools
from typing import Any, NamedTuple
import jax
import jax.numpy as jnp
from jax import lax
from jax.sharding import PartitionSpec as P
from jax.experimental import pallas as pl
from jax.experimental.pallas import tpu as pltpu

ITERS = 8
RIDGE = 1.0
CHUNK = 512
PICK = 128
MESH = pl.DeviceIdType.MESH
F32 = jnp.float32
BF16 = jnp.bfloat16


def split2(value):
    high = value.astype(BF16)
    return high, (value - high.astype(F32)).astype(BF16)


def split3(value):
    high = value.astype(BF16)
    rest = value - high.astype(F32)
    middle = rest.astype(BF16)
    return high, middle, (rest - middle.astype(F32)).astype(BF16)


def dot(left, right):
    return jnp.dot(left, right, preferred_element_type=F32)


def halves(value):
    width = value.shape[1] // 2
    return value[:, :width] + value[:, width:]


def iota(shape, axis):
    return lax.broadcasted_iota(jnp.int32, shape, axis)


def owner_table(first, rows, capacity, senders):
    owner = lax.div(iota((rows, senders), 0), capacity) + first
    return (owner == iota((rows, senders), 1)).astype(F32).astype(BF16)


def spread(pieces, first, rows, capacity, senders):
    table = owner_table(first, rows, capacity, senders)
    wide = halves(dot(table, jnp.concatenate(pieces[:2], axis=1)))
    if len(pieces) > 2:
        wide = wide + dot(table, pieces[2])
    return wide


def column(wide, which, capacity):
    slot = lax.rem(iota(wide.shape, 0), capacity) + which * capacity
    return jnp.sum(jnp.where(slot == iota(wide.shape, 1), wide, 0.0), axis=1, keepdims=True)


def row_table(indices, groups, capacity, out):
    senders = indices.shape[1]
    both = jnp.concatenate(split2(indices), axis=0)
    slots = senders * capacity
    for first in range(0, slots, CHUNK):
        owner = lax.div(iota((senders, CHUNK), 1), capacity) + first // capacity
        table = (owner == iota((senders, CHUNK), 0)).astype(F32).astype(BF16)
        wide = dot(both, table)
        wide = wide[:capacity] + wide[capacity:]
        mine = iota(wide.shape, 0) == lax.rem(iota(wide.shape, 1), capacity)
        row = jnp.sum(jnp.where(mine, wide, 0.0), axis=0, keepdims=True).astype(jnp.int32)
        hot = (row == iota((groups, CHUNK), 0)).astype(F32).astype(BF16)
        out[:, pl.ds(first, CHUNK)] = hot


def column_table(wide, which, capacity, groups):
    index = column(wide, which, capacity).astype(jnp.int32)
    return (index == iota((wide.shape[0], groups), 1)).astype(F32).astype(BF16)


def set_gram(gram, pair, single):
    rank = gram.shape[0]
    ridge = jnp.where(iota((rank, rank), 0) == iota((rank, rank), 1), RIDGE, 0.0)
    high, middle, low = split3(gram + ridge)
    pair[...] = jnp.concatenate(
        [jnp.concatenate([high, middle], axis=1), jnp.concatenate([middle, high], axis=1)], axis=0
    )
    single[...] = jnp.concatenate([low, high], axis=0)


class State(NamedTuple):
    x: Any
    r: Any
    p: Any
    squares: Any
    pieces: Any
    terms: Any
    pair: Any
    single: Any
    block: int


def pick_terms(state, rows_ref, scaled, coefs, hot):
    slots, rank = scaled.shape
    capacity = rows_ref.shape[1]
    for first in range(0, slots, PICK):
        part = pl.ds(first, PICK)
        rows = rows_ref[pl.ds(first // capacity, PICK // capacity)].reshape(PICK, rank)
        picked = halves(dot(hot[part, :], state.pieces[:, : 2 * rank]))
        along = jnp.sum(rows * picked, axis=1, keepdims=True)
        if coefs is None:
            terms = along * scaled[part, :]
        else:
            weighted = scaled[part, :] * rows
            scaled[part, :] = weighted
            terms = coefs[part, :] * rows - along * weighted
        high, low = split2(terms)
        state.terms[part, :rank] = high
        state.terms[part, rank:] = low


def keep_pieces(state, part, value):
    rank = value.shape[1]
    for index, piece in enumerate(split3(value)):
        state.pieces[part, index * rank : (index + 1) * rank] = piece


def gram_part(state, part, rank):
    mine = state.pieces[part, :]
    first = dot(mine[:, : 2 * rank], state.pair[...])
    outer = jnp.concatenate([mine[:, :rank], mine[:, 2 * rank :]], axis=1)
    return halves(first) + dot(outer, state.single[...])


def fold_start(state, base, hot_t):
    groups = state.x.shape[0]
    for first in range(0, groups, state.block):
        part = pl.ds(first, state.block)
        r = halves(dot(hot_t[part, :], state.terms[...]))
        if base is not None:
            r = r + base[part, :]
        state.r[part, :] = r


def conjugate_steps(state, rows_ref, scaled, hot, hot_t):
    groups, rank = state.x.shape
    for first in range(0, groups, state.block):
        part = pl.ds(first, state.block)
        r = state.r[part, :] - gram_part(state, part, rank)
        state.r[part, :] = r
        state.p[part, :] = r
        squares = jnp.sum(r * r, axis=1, keepdims=True)
        state.squares[part, :] = jnp.broadcast_to(squares, r.shape)
        keep_pieces(state, part, r)

    def step(last):
        pick_terms(state, rows_ref, scaled, None, hot)
        for first in range(0, groups, state.block):
            part = pl.ds(first, state.block)
            image = halves(dot(hot_t[part, :], state.terms[...])) + gram_part(state, part, rank)
            p = state.p[part, :]
            squares = state.squares[part, :]
            alpha = squares / jnp.sum(p * image, axis=1, keepdims=True)
            x = state.x[part, :] + alpha * p
            state.x[part, :] = x
            if last:
                keep_pieces(state, part, x)
                continue
            r = state.r[part, :] - alpha * image
            state.r[part, :] = r
            fresh = jnp.sum(r * r, axis=1, keepdims=True)
            p = r + (fresh / squares) * p
            state.p[part, :] = p
            state.squares[part, :] = jnp.broadcast_to(fresh, p.shape)
            keep_pieces(state, part, p)

    def middle(iteration, carry):
        step(False)
        return carry

    lax.fori_loop(0, ITERS - 1, middle, 0)
    step(True)


def body(
    n,
    fast,
    capacity,
    user_in,
    item_in,
    rhs_in,
    user_gram_in,
    count_in,
    asked_in,
    members_in,
    weight_in,
    rating_in,
    user_out,
    item_out,
    item_v,
    rhs_v,
    user_gram,
    count_v,
    asked_v,
    members_v,
    weight_v,
    rating_v,
    note_src,
    gathered,
    relay,
    notes,
    partial,
    near,
    across,
    whole,
    part_src,
    parts,
    row_src,
    gram_rows,
    found,
    fetched,
    outgoing,
    arrived,
    user_scaled,
    user_coefs,
    item_scaled,
    item_coefs,
    user_hot,
    user_hot_t,
    item_hot,
    item_hot_t,
    pair,
    single,
    terms,
    user_r,
    user_p,
    user_squares,
    user_pieces,
    item_r,
    item_p,
    item_squares,
    item_pieces,
    send_sem,
    recv_sem,
    own_sem,
    load_sem,
):
    me = lax.axis_index("users") * fast + lax.axis_index("items")
    slots = n * capacity
    users, rank = user_out.shape
    items = item_out.shape[0]
    inner = near.shape[0]
    outer = across.shape[0]
    band = rank // inner
    seat, team = lax.rem(me, inner), lax.div(me, inner)
    region = CHUNK // capacity
    barrier = pltpu.get_barrier_semaphore()

    loads = [
        pltpu.make_async_copy(source, target, load_sem.at[index])
        for index, (source, target) in enumerate(
            (
                (count_in, count_v),
                (asked_in, asked_v),
                (members_in, members_v),
                (weight_in, weight_v),
                (rating_in, rating_v),
                (item_in, item_v),
                (user_in, user_out),
                (rhs_in, rhs_v),
                (user_gram_in, user_gram),
                (item_in, item_out),
            )
        )
    ]
    for load in loads:
        load.start()

    def at(peer):
        return (lax.div(peer, fast), lax.rem(peer, fast))

    def mate(step):
        return team * inner + lax.rem(seat + step, inner)

    def counterpart(step):
        return lax.rem(team + step, outer) * inner + seat

    for count, other in ((inner, mate), (outer, counterpart)):

        @pl.loop(1, count)
        def _(step):
            pl.semaphore_signal(barrier, inc=1, device_id=at(other(step)), device_id_type=MESH)

    def push(which, source, target, peer):
        pltpu.make_async_remote_copy(
            src_ref=source,
            dst_ref=target,
            send_sem=send_sem.at[which],
            recv_sem=recv_sem.at[which],
            device_id=at(peer),
            device_id_type=MESH,
        ).start()

    def landed(which, target):
        span = target.at[pl.ds(0, target.shape[0] - 1)]
        pltpu.make_async_copy(span, span, recv_sem.at[which]).wait()

    def sent(which, target):
        span = target.at[pl.ds(0, target.shape[0] - 1)]
        pltpu.make_async_copy(span, span, send_sem.at[which]).wait()

    def own(which, source, target):
        return pltpu.make_async_copy(source.at[me], target.at[me], own_sem.at[which])

    def gram_near(which, source, first):
        first[seat] = source[pl.ds(pl.multiple_of(seat * band, band), band), :]

        @pl.loop(1, inner)
        def _(step):
            other = lax.rem(seat + step, inner)
            push(
                which,
                source.at[pl.ds(pl.multiple_of(other * band, band), band)],
                first.at[seat],
                team * inner + other,
            )

    def give_back(which, third):
        @pl.loop(1, inner)
        def _(step):
            other = lax.rem(seat + step, inner)
            push(which, third.at[seat], third.at[seat], team * inner + other)

    def send_region(which, source, target, base):
        @pl.loop(0, region)
        def _(step):
            peer = base + lax.rem(me + step, region)

            @pl.when(peer != me)
            def _():
                push(which, source.at[peer], target.at[me], peer)

    def turn(step):
        return lax.rem(lax.axis_index("items") + step, slots // CHUNK)

    for load in loads[:5]:
        load.wait()
    live = iota((capacity, n), 0) < count_v[...]
    weights = jnp.where(live, weight_v[...], 0.0)
    coefs = jnp.where(live, (1.0 + weight_v[...]) * rating_v[...], 0.0)
    asked = asked_v[...].astype(F32)
    members = members_v[...].astype(F32)
    rest = jnp.zeros((rank - 4 * capacity, n), F32)
    own_note = jnp.concatenate([asked, weights, coefs, members, rest], axis=0).T
    for index in range(outer):
        note_src[:, index, :] = own_note[index * inner : (index + 1) * inner]
    pl.semaphore_wait(barrier, inner + outer - 2)

    @pl.loop(1, inner)
    def _(step):
        other = lax.rem(seat + step, inner)
        push(0, note_src.at[other], gathered.at[seat], mate(step))

    gathered[seat] = note_src[seat]
    loads[5].wait()
    mine = item_v[...]
    partial[...] = jnp.dot(
        mine.T, mine, precision=lax.Precision.HIGHEST, preferred_element_type=F32
    )
    gram_near(5, partial, near)
    landed(0, gathered)
    for index in range(outer):
        relay[index] = gathered[:, index, :]

    @pl.loop(1, outer)
    def _(step):
        other = lax.rem(team + step, outer)
        push(6, relay.at[other], notes.at[team], counterpart(step))

    notes[team] = relay[team]
    landed(5, near)
    across[team] = jnp.sum(near[...], axis=0)

    @pl.loop(1, outer)
    def _(step):
        push(7, across.at[team], across.at[team], counterpart(step))

    user_state = State(
        user_out, user_r, user_p, user_squares, user_pieces, terms, pair, single, users // 2
    )
    item_state = State(
        item_out, item_r, item_p, item_squares, item_pieces, terms, pair, single, items // 2
    )
    keep_pieces(item_state, slice(None), item_v[...])

    landed(6, notes)
    all_notes = notes[...].reshape(n, rank)
    pieces = split3(all_notes)
    for step in range(slots // CHUNK):
        base = pl.multiple_of(turn(step) * region, region)
        wide = spread(pieces[:2], base, CHUNK, capacity, n)
        hot = column_table(wide, 0, capacity, items)
        item_hot[pl.ds(pl.multiple_of(base * capacity, CHUNK), CHUNK), :] = hot
        picked = halves(dot(hot, item_pieces[:, : 2 * rank]))
        picked = picked + dot(hot, item_pieces[:, 2 * rank :])
        found[pl.ds(base, region)] = picked.reshape(region, capacity, rank)
        send_region(1, found, fetched, base)
        if step == 0:
            landed(7, across)
            whole[seat] = jnp.sum(across[...], axis=0)
            give_back(8, whole)
    own(1, found, fetched).start()

    own_pieces = split3(own_note)
    for first in range(0, slots, CHUNK):
        part = pl.ds(first, CHUNK)
        wide = spread(own_pieces, first // capacity, CHUNK, capacity, n)
        user_scaled[part, :] = jnp.broadcast_to(column(wide, 1, capacity), (CHUNK, rank))
        user_coefs[part, :] = jnp.broadcast_to(column(wide, 2, capacity), (CHUNK, rank))
        user_hot[part, :] = column_table(wide, 3, capacity, users)
    row_table(members, users, capacity, user_hot_t)
    loads[6].wait()
    for first in range(0, slots, CHUNK):
        part = pl.ds(first, CHUNK)
        wide = spread(pieces, first // capacity, CHUNK, capacity, n)
        item_scaled[part, :] = jnp.broadcast_to(column(wide, 1, capacity), (CHUNK, rank))
        item_coefs[part, :] = jnp.broadcast_to(column(wide, 2, capacity), (CHUNK, rank))
    row_table(all_notes.T[:capacity], items, capacity, item_hot_t)

    keep_pieces(user_state, slice(None), user_out[...])
    own(1, found, fetched).wait()
    landed(1, fetched)
    pick_terms(user_state, fetched, user_scaled, user_coefs, user_hot)
    fold_start(user_state, None, user_hot_t)
    landed(8, whole)
    set_gram(whole[...].reshape(rank, rank), pair, single)
    conjugate_steps(user_state, fetched, user_scaled, user_hot, user_hot_t)

    for step in range(slots // CHUNK):
        base = pl.multiple_of(turn(step) * region, region)
        hot = user_hot[pl.ds(pl.multiple_of(base * capacity, CHUNK), CHUNK), :]
        picked = halves(dot(hot, user_pieces[:, : 2 * rank]))
        picked = picked + dot(hot, user_pieces[:, 2 * rank :])
        outgoing[pl.ds(base, region)] = picked.reshape(region, capacity, rank)
        send_region(2, outgoing, arrived, base)
        if step == 0:
            refreshed = user_out[...]
            gram = jnp.dot(
                refreshed.T,
                refreshed,
                precision=lax.Precision.HIGHEST,
                preferred_element_type=F32,
            )
            part_src[...] = gram[:, None, :]
            parts[me] = part_src[me]

            @pl.loop(1, n)
            def _(step):
                peer = lax.rem(me + step, n)
                push(3, part_src.at[peer], parts.at[me], peer)

    own(2, outgoing, arrived).start()
    landed(3, parts)
    row = jnp.sum(parts[...], axis=0)
    row_src[0] = row
    gram_rows[me] = row

    @pl.loop(1, n)
    def _(step):
        push(4, row_src.at[0], gram_rows.at[me], lax.rem(me + step, n))


    for load in loads[7:]:
        load.wait()
    own(2, outgoing, arrived).wait()
    landed(2, arrived)
    pick_terms(item_state, arrived, item_scaled, item_coefs, item_hot)
    fold_start(item_state, rhs_v, item_hot_t)
    landed(4, gram_rows)
    set_gram(user_gram[...] + gram_rows[:, 0, :], pair, single)
    conjugate_steps(item_state, arrived, item_scaled, item_hot, item_hot_t)
    for which, target in enumerate(
        (gathered, fetched, arrived, parts, gram_rows, near, notes, across, whole)
    ):
        sent(which, target)


def hand_on(user_in, item_in, user_out, item_out, sems):
    moves = [
        pltpu.make_async_copy(item_in, item_out, sems.at[0]),
        pltpu.make_async_copy(user_in, user_out, sems.at[1]),
    ]
    for move in moves:
        move.start()
    for move in moves:
        move.wait()


def per_device(
    user_old, item_old, item_rhs, user_gram, req_count, req_item, req_user, weight, rating
):
    fast = lax.axis_size("items")
    n = lax.axis_size("users") * fast
    capacity = req_item.shape[2]
    users, rank = user_old.shape
    items = item_old.shape[0]
    slots = n * capacity
    inner = 2 * fast
    outer = n // inner
    anywhere = pl.BlockSpec(memory_space=pl.ANY)
    vmem = pl.BlockSpec(memory_space=pltpu.VMEM)

    def floats(*shape):
        return pltpu.VMEM(shape, F32)

    gram = [
        floats(rank, rank),
        floats(inner, rank // inner, rank),
        floats(outer, rank // inner, rank),
        floats(inner, rank // inner, rank),
    ]
    flip = lambda array: jnp.swapaxes(array[0], 0, 1)
    results = pl.pallas_call(
        functools.partial(body, n, fast, capacity),
        out_shape=(floats(users, rank), floats(items, rank)),
        in_specs=[anywhere] * 9,
        out_specs=(vmem, vmem),
        scratch_shapes=[
            floats(items, rank),
            floats(items, rank),
            floats(rank, rank),
            pltpu.VMEM((1, n), jnp.int32),
            pltpu.VMEM((capacity, n), jnp.int32),
            pltpu.VMEM((capacity, n), jnp.int32),
            floats(capacity, n),
            floats(capacity, n),
            floats(inner, outer, rank),
            floats(inner, outer, rank),
            floats(outer, inner, rank),
            floats(outer, inner, rank),
            *gram,
            floats(n, 1, rank),
            floats(n, 1, rank),
            floats(1, 1, rank),
            floats(n, 1, rank),
            *[floats(n, capacity, rank)] * 4,
            *[floats(slots, rank)] * 4,
            pltpu.VMEM((slots, users), BF16),
            pltpu.VMEM((users, slots), BF16),
            pltpu.VMEM((slots, items), BF16),
            pltpu.VMEM((items, slots), BF16),
            pltpu.VMEM((2 * rank, 2 * rank), BF16),
            pltpu.VMEM((2 * rank, rank), BF16),
            pltpu.VMEM((slots, 2 * rank), BF16),
            *[floats(users, rank)] * 3,
            pltpu.VMEM((users, 3 * rank), BF16),
            *[floats(items, rank)] * 3,
            pltpu.VMEM((items, 3 * rank), BF16),
            pltpu.SemaphoreType.DMA((9,)),
            pltpu.SemaphoreType.DMA((9,)),
            pltpu.SemaphoreType.DMA((3,)),
            pltpu.SemaphoreType.DMA((10,)),
        ],
        compiler_params=pltpu.CompilerParams(
            collective_id=0, has_side_effects=True, vmem_limit_bytes=60 * 2**20
        ),
    )(
        user_old,
        item_old,
        item_rhs,
        user_gram,
        req_count,
        flip(req_item),
        flip(req_user),
        flip(weight),
        flip(rating),
    )
    return pl.pallas_call(
        hand_on,
        out_shape=tuple(jax.ShapeDtypeStruct(array.shape, F32) for array in results),
        in_specs=[vmem] * 2,
        out_specs=(anywhere, anywhere),
        scratch_shapes=[pltpu.SemaphoreType.DMA((2,))],
        compiler_params=pltpu.CompilerParams(vmem_limit_bytes=2 * 2**20),
    )(*results)


def solution(mesh):
    in_specs = (
        P(("users", "items"), None),
        P(("users", "items"), None),
        P(("users", "items"), None),
        P(),
        P(("users", "items"), None),
        P(("users", "items"), None, None),
        P(("users", "items"), None, None),
        P(("users", "items"), None, None),
        P(("users", "items"), None, None),
    )
    out_specs = (P(("users", "items"), None), P(("users", "items"), None))
    return jax.shard_map(
        per_device, mesh=mesh, in_specs=in_specs, out_specs=out_specs, check_vma=False
    )
```

```python
import functools
from typing import Any, NamedTuple
import jax
import jax.numpy as jnp
from jax import lax
from jax.sharding import PartitionSpec as P
from jax.experimental import pallas as pl
from jax.experimental.pallas import tpu as pltpu

ITERS = 8
RIDGE = 1.0
CHUNK = 512
PICK = 128
FLAT = pl.DeviceIdType.LOGICAL
F32 = jnp.float32
BF16 = jnp.bfloat16


def split2(value):
    high = value.astype(BF16)
    return high, (value - high.astype(F32)).astype(BF16)


def split3(value):
    high = value.astype(BF16)
    rest = value - high.astype(F32)
    middle = rest.astype(BF16)
    return high, middle, (rest - middle.astype(F32)).astype(BF16)


def dot(left, right):
    return jnp.dot(left, right, preferred_element_type=F32)


def halves(value):
    width = value.shape[1] // 2
    return value[:, :width] + value[:, width:]


def iota(shape, axis):
    return lax.broadcasted_iota(jnp.int32, shape, axis)


def owner_table(first, rows, capacity, senders):
    owner = lax.div(iota((rows, senders), 0), capacity) + first
    return (owner == iota((rows, senders), 1)).astype(F32).astype(BF16)


def spread(pieces, first, rows, capacity, senders):
    table = owner_table(first, rows, capacity, senders)
    wide = halves(dot(table, jnp.concatenate(pieces[:2], axis=1)))
    if len(pieces) > 2:
        wide = wide + dot(table, pieces[2])
    return wide


def column(wide, which, capacity):
    slot = lax.rem(iota(wide.shape, 0), capacity) + which * capacity
    return jnp.sum(jnp.where(slot == iota(wide.shape, 1), wide, 0.0), axis=1, keepdims=True)


def row_table(indices, groups, capacity, out):
    senders = indices.shape[1]
    both = jnp.concatenate(split2(indices), axis=0)
    slots = senders * capacity
    for first in range(0, slots, CHUNK):
        owner = lax.div(iota((senders, CHUNK), 1), capacity) + first // capacity
        table = (owner == iota((senders, CHUNK), 0)).astype(F32).astype(BF16)
        wide = dot(both, table)
        wide = wide[:capacity] + wide[capacity:]
        mine = iota(wide.shape, 0) == lax.rem(iota(wide.shape, 1), capacity)
        row = jnp.sum(jnp.where(mine, wide, 0.0), axis=0, keepdims=True).astype(jnp.int32)
        hot = (row == iota((groups, CHUNK), 0)).astype(F32).astype(BF16)
        out[:, pl.ds(first, CHUNK)] = hot


def column_table(wide, which, capacity, groups):
    index = column(wide, which, capacity).astype(jnp.int32)
    return (index == iota((wide.shape[0], groups), 1)).astype(F32).astype(BF16)


def set_gram(gram, pair, single):
    rank = gram.shape[0]
    ridge = jnp.where(iota((rank, rank), 0) == iota((rank, rank), 1), RIDGE, 0.0)
    high, middle, low = split3(gram + ridge)
    pair[...] = jnp.concatenate(
        [jnp.concatenate([high, middle], axis=1), jnp.concatenate([middle, high], axis=1)], axis=0
    )
    single[...] = jnp.concatenate([low, high], axis=0)


class State(NamedTuple):
    x: Any
    r: Any
    p: Any
    squares: Any
    pieces: Any
    terms: Any
    pair: Any
    single: Any
    block: int


def pick_terms(state, rows_ref, scaled, coefs, hot):
    slots, rank = scaled.shape
    capacity = rows_ref.shape[1]
    for first in range(0, slots, PICK):
        part = pl.ds(first, PICK)
        rows = rows_ref[pl.ds(first // capacity, PICK // capacity)].reshape(PICK, rank)
        picked = halves(dot(hot[part, :], state.pieces[:, : 2 * rank]))
        along = jnp.sum(rows * picked, axis=1, keepdims=True)
        if coefs is None:
            terms = along * scaled[part, :]
        else:
            weighted = scaled[part, :] * rows
            scaled[part, :] = weighted
            terms = coefs[part, :] * rows - along * weighted
        high, low = split2(terms)
        state.terms[part, :rank] = high
        state.terms[part, rank:] = low


def keep_pieces(state, part, value):
    rank = value.shape[1]
    for index, piece in enumerate(split3(value)):
        state.pieces[part, index * rank : (index + 1) * rank] = piece


def gram_part(state, part, rank, full=True):
    mine = state.pieces[part, :]
    first = dot(mine[:, : 2 * rank], state.pair[...])
    if not full:
        return halves(first)
    outer = jnp.concatenate([mine[:, :rank], mine[:, 2 * rank :]], axis=1)
    return halves(first) + dot(outer, state.single[...])


def fold_start(state, base, hot_t):
    groups = state.x.shape[0]
    for first in range(0, groups, state.block):
        part = pl.ds(first, state.block)
        r = halves(dot(hot_t[part, :], state.terms[...]))
        if base is not None:
            r = r + base[part, :]
        state.r[part, :] = r


def conjugate_steps(state, rows_ref, scaled, hot, hot_t, exact):
    groups, rank = state.x.shape
    for first in range(0, groups, state.block):
        part = pl.ds(first, state.block)
        r = state.r[part, :] - gram_part(state, part, rank)
        state.r[part, :] = r
        state.p[part, :] = r
        squares = jnp.sum(r * r, axis=1, keepdims=True)
        state.squares[part, :] = jnp.broadcast_to(squares, r.shape)
        keep_pieces(state, part, r)

    def step(last, full):
        pick_terms(state, rows_ref, scaled, None, hot)
        for first in range(0, groups, state.block):
            part = pl.ds(first, state.block)
            image = halves(dot(hot_t[part, :], state.terms[...]))
            image = image + gram_part(state, part, rank, full)
            p = state.p[part, :]
            squares = state.squares[part, :]
            alpha = squares / jnp.sum(p * image, axis=1, keepdims=True)
            x = state.x[part, :] + alpha * p
            state.x[part, :] = x
            if last:
                keep_pieces(state, part, x)
                continue
            r = state.r[part, :] - alpha * image
            state.r[part, :] = r
            fresh = jnp.sum(r * r, axis=1, keepdims=True)
            p = r + (fresh / squares) * p
            state.p[part, :] = p
            state.squares[part, :] = jnp.broadcast_to(fresh, p.shape)
            keep_pieces(state, part, p)

    def middle(full, iteration, carry):
        step(False, full)
        return carry

    lax.fori_loop(0, exact, functools.partial(middle, True), 0)
    if exact < ITERS - 1:
        lax.fori_loop(exact, ITERS - 1, functools.partial(middle, False), 0)
    step(True, exact == ITERS - 1)


def body(
    n,
    fast,
    capacity,
    user_in,
    item_in,
    rhs_in,
    user_gram_in,
    count_in,
    asked_in,
    members_in,
    weight_in,
    rating_in,
    user_out,
    item_out,
    item_v,
    rhs_v,
    user_gram,
    count_v,
    asked_v,
    members_v,
    weight_v,
    rating_v,
    note_src,
    gathered,
    relay,
    notes,
    partial,
    near,
    across,
    whole,
    part_src,
    parts,
    row_src,
    gram_rows,
    found,
    fetched,
    outgoing,
    arrived,
    user_scaled,
    user_coefs,
    item_scaled,
    item_coefs,
    user_hot,
    user_hot_t,
    item_hot,
    item_hot_t,
    pair,
    single,
    terms,
    user_r,
    user_p,
    user_squares,
    user_pieces,
    item_r,
    item_p,
    item_squares,
    item_pieces,
    send_sem,
    recv_sem,
    own_sem,
    load_sem,
):
    me = lax.axis_index("users") * fast + lax.axis_index("items")
    slots = n * capacity
    users, rank = user_out.shape
    items = item_out.shape[0]
    inner = near.shape[0]
    outer = across.shape[0]
    band = rank // inner
    seat, team = lax.rem(me, inner), lax.div(me, inner)
    region = CHUNK // capacity
    barrier = pltpu.get_barrier_semaphore()

    loads = [
        pltpu.make_async_copy(source, target, load_sem.at[index])
        for index, (source, target) in enumerate(
            (
                (count_in, count_v),
                (asked_in, asked_v),
                (members_in, members_v),
                (weight_in, weight_v),
                (rating_in, rating_v),
                (item_in, item_v),
                (user_in, user_out),
                (rhs_in, rhs_v),
                (user_gram_in, user_gram),
                (item_in, item_out),
            )
        )
    ]
    for load in loads:
        load.start()

    def mate(step):
        return team * inner + lax.rem(seat + step, inner)

    def counterpart(step):
        return lax.rem(team + step, outer) * inner + seat

    for count, other in ((inner, mate), (outer, counterpart)):

        @pl.loop(1, count)
        def _(step):
            pl.semaphore_signal(barrier, inc=1, device_id=other(step), device_id_type=FLAT)

    def push(which, source, target, peer):
        pltpu.make_async_remote_copy(
            src_ref=source,
            dst_ref=target,
            send_sem=send_sem.at[which],
            recv_sem=recv_sem.at[which],
            device_id=peer,
            device_id_type=FLAT,
        ).start()

    def landed(which, target):
        span = target.at[pl.ds(0, target.shape[0] - 1)]
        pltpu.make_async_copy(span, span, recv_sem.at[which]).wait()

    def sent(which, target):
        span = target.at[pl.ds(0, target.shape[0] - 1)]
        pltpu.make_async_copy(span, span, send_sem.at[which]).wait()

    def own(which, source, target):
        return pltpu.make_async_copy(source.at[me], target.at[me], own_sem.at[which])

    def gram_near(which, source, first):
        first[seat] = source[pl.ds(pl.multiple_of(seat * band, band), band), :]

        @pl.loop(1, inner)
        def _(step):
            other = lax.rem(seat + step, inner)
            push(
                which,
                source.at[pl.ds(pl.multiple_of(other * band, band), band)],
                first.at[seat],
                team * inner + other,
            )

    def give_back(which, third):
        @pl.loop(1, inner)
        def _(step):
            other = lax.rem(seat + step, inner)
            push(which, third.at[seat], third.at[seat], team * inner + other)

    def send_region(which, source, target, base):
        @pl.loop(0, region)
        def _(step):
            peer = base + lax.rem(me + step, region)

            @pl.when(peer != me)
            def _():
                push(which, source.at[peer], target.at[me], peer)

    def turn(step):
        return lax.rem(lax.axis_index("items") + step, slots // CHUNK)

    for load in loads[:5]:
        load.wait()
    live = iota((capacity, n), 0) < count_v[...]
    weights = jnp.where(live, weight_v[...], 0.0)
    coefs = jnp.where(live, (1.0 + weight_v[...]) * rating_v[...], 0.0)
    asked = asked_v[...].astype(F32)
    members = members_v[...].astype(F32)
    rest = jnp.zeros((rank - 4 * capacity, n), F32)
    own_note = jnp.concatenate([asked, weights, coefs, members, rest], axis=0).T
    for index in range(outer):
        note_src[:, index, :] = own_note[index * inner : (index + 1) * inner]
    pl.semaphore_wait(barrier, inner + outer - 2)

    @pl.loop(1, inner)
    def _(step):
        other = lax.rem(seat + step, inner)
        push(0, note_src.at[other], gathered.at[seat], mate(step))

    gathered[seat] = note_src[seat]
    loads[5].wait()
    mine = item_v[...]
    partial[...] = jnp.dot(
        mine.T, mine, precision=lax.Precision.HIGHEST, preferred_element_type=F32
    )
    gram_near(5, partial, near)
    landed(0, gathered)
    for index in range(outer):
        relay[index] = gathered[:, index, :]

    @pl.loop(1, outer)
    def _(step):
        other = lax.rem(team + step, outer)
        push(6, relay.at[other], notes.at[team], counterpart(step))

    notes[team] = relay[team]
    landed(5, near)
    across[team] = jnp.sum(near[...], axis=0)

    @pl.loop(1, outer)
    def _(step):
        push(7, across.at[team], across.at[team], counterpart(step))

    user_state = State(
        user_out, user_r, user_p, user_squares, user_pieces, terms, pair, single, users // 2
    )
    item_state = State(
        item_out, item_r, item_p, item_squares, item_pieces, terms, pair, single, items // 2
    )
    keep_pieces(item_state, slice(None), item_v[...])

    landed(6, notes)
    all_notes = notes[...].reshape(n, rank)
    pieces = split3(all_notes)
    for step in range(slots // CHUNK):
        base = pl.multiple_of(turn(step) * region, region)
        wide = spread(pieces[:2], base, CHUNK, capacity, n)
        hot = column_table(wide, 0, capacity, items)
        item_hot[pl.ds(pl.multiple_of(base * capacity, CHUNK), CHUNK), :] = hot
        picked = halves(dot(hot, item_pieces[:, : 2 * rank]))
        picked = picked + dot(hot, item_pieces[:, 2 * rank :])
        found[pl.ds(base, region)] = picked.reshape(region, capacity, rank)
        send_region(1, found, fetched, base)
        if step == 0:
            landed(7, across)
            whole[seat] = jnp.sum(across[...], axis=0)
            give_back(8, whole)
    own(1, found, fetched).start()

    own_pieces = split3(own_note)
    for first in range(0, slots, CHUNK):
        part = pl.ds(first, CHUNK)
        wide = spread(own_pieces, first // capacity, CHUNK, capacity, n)
        user_scaled[part, :] = jnp.broadcast_to(column(wide, 1, capacity), (CHUNK, rank))
        user_coefs[part, :] = jnp.broadcast_to(column(wide, 2, capacity), (CHUNK, rank))
        user_hot[part, :] = column_table(wide, 3, capacity, users)
    row_table(members, users, capacity, user_hot_t)
    loads[6].wait()
    for first in range(0, slots, CHUNK):
        part = pl.ds(first, CHUNK)
        wide = spread(pieces, first // capacity, CHUNK, capacity, n)
        item_scaled[part, :] = jnp.broadcast_to(column(wide, 1, capacity), (CHUNK, rank))
        item_coefs[part, :] = jnp.broadcast_to(column(wide, 2, capacity), (CHUNK, rank))
    row_table(all_notes.T[:capacity], items, capacity, item_hot_t)

    keep_pieces(user_state, slice(None), user_out[...])
    own(1, found, fetched).wait()
    landed(1, fetched)
    pick_terms(user_state, fetched, user_scaled, user_coefs, user_hot)
    fold_start(user_state, None, user_hot_t)
    landed(8, whole)
    set_gram(whole[...].reshape(rank, rank), pair, single)
    conjugate_steps(user_state, fetched, user_scaled, user_hot, user_hot_t, ITERS - 1)

    for step in range(slots // CHUNK):
        base = pl.multiple_of(turn(step) * region, region)
        hot = user_hot[pl.ds(pl.multiple_of(base * capacity, CHUNK), CHUNK), :]
        picked = halves(dot(hot, user_pieces[:, : 2 * rank]))
        picked = picked + dot(hot, user_pieces[:, 2 * rank :])
        outgoing[pl.ds(base, region)] = picked.reshape(region, capacity, rank)
        send_region(2, outgoing, arrived, base)
        if step == 0:
            refreshed = user_out[...]
            gram = jnp.dot(
                refreshed.T,
                refreshed,
                precision=lax.Precision.HIGHEST,
                preferred_element_type=F32,
            )
            part_src[...] = gram[:, None, :]
            parts[me] = part_src[me]

            @pl.loop(1, n)
            def _(step):
                peer = lax.rem(me + step, n)
                push(3, part_src.at[peer], parts.at[me], peer)

    own(2, outgoing, arrived).start()
    landed(3, parts)
    row = jnp.sum(parts[...], axis=0)
    row_src[0] = row
    gram_rows[me] = row

    @pl.loop(1, n)
    def _(step):
        push(4, row_src.at[0], gram_rows.at[me], lax.rem(me + step, n))


    for load in loads[7:]:
        load.wait()
    own(2, outgoing, arrived).wait()
    landed(2, arrived)
    pick_terms(item_state, arrived, item_scaled, item_coefs, item_hot)
    fold_start(item_state, rhs_v, item_hot_t)
    landed(4, gram_rows)
    set_gram(user_gram[...] + gram_rows[:, 0, :], pair, single)
    conjugate_steps(item_state, arrived, item_scaled, item_hot, item_hot_t, ITERS // 2)
    for which, target in enumerate(
        (gathered, fetched, arrived, parts, gram_rows, near, notes, across, whole)
    ):
        sent(which, target)


def hand_on(user_in, item_in, user_out, item_out, sems):
    moves = [
        pltpu.make_async_copy(item_in, item_out, sems.at[0]),
        pltpu.make_async_copy(user_in, user_out, sems.at[1]),
    ]
    for move in moves:
        move.start()
    for move in moves:
        move.wait()


def per_device(
    user_old, item_old, item_rhs, user_gram, req_count, req_item, req_user, weight, rating
):
    fast = lax.axis_size("items")
    n = lax.axis_size("users") * fast
    capacity = req_item.shape[2]
    users, rank = user_old.shape
    items = item_old.shape[0]
    slots = n * capacity
    inner = 2 * fast
    outer = n // inner
    anywhere = pl.BlockSpec(memory_space=pl.ANY)
    vmem = pl.BlockSpec(memory_space=pltpu.VMEM)

    def floats(*shape):
        return pltpu.VMEM(shape, F32)

    gram = [
        floats(rank, rank),
        floats(inner, rank // inner, rank),
        floats(outer, rank // inner, rank),
        floats(inner, rank // inner, rank),
    ]
    flip = lambda array: jnp.swapaxes(array[0], 0, 1)
    results = pl.pallas_call(
        functools.partial(body, n, fast, capacity),
        out_shape=(floats(users, rank), floats(items, rank)),
        in_specs=[anywhere] * 9,
        out_specs=(vmem, vmem),
        scratch_shapes=[
            floats(items, rank),
            floats(items, rank),
            floats(rank, rank),
            pltpu.VMEM((1, n), jnp.int32),
            pltpu.VMEM((capacity, n), jnp.int32),
            pltpu.VMEM((capacity, n), jnp.int32),
            floats(capacity, n),
            floats(capacity, n),
            floats(inner, outer, rank),
            floats(inner, outer, rank),
            floats(outer, inner, rank),
            floats(outer, inner, rank),
            *gram,
            floats(n, 1, rank),
            floats(n, 1, rank),
            floats(1, 1, rank),
            floats(n, 1, rank),
            *[floats(n, capacity, rank)] * 4,
            *[floats(slots, rank)] * 4,
            pltpu.VMEM((slots, users), BF16),
            pltpu.VMEM((users, slots), BF16),
            pltpu.VMEM((slots, items), BF16),
            pltpu.VMEM((items, slots), BF16),
            pltpu.VMEM((2 * rank, 2 * rank), BF16),
            pltpu.VMEM((2 * rank, rank), BF16),
            pltpu.VMEM((slots, 2 * rank), BF16),
            *[floats(users, rank)] * 3,
            pltpu.VMEM((users, 3 * rank), BF16),
            *[floats(items, rank)] * 3,
            pltpu.VMEM((items, 3 * rank), BF16),
            pltpu.SemaphoreType.DMA((9,)),
            pltpu.SemaphoreType.DMA((9,)),
            pltpu.SemaphoreType.DMA((3,)),
            pltpu.SemaphoreType.DMA((10,)),
        ],
        compiler_params=pltpu.CompilerParams(
            collective_id=0, has_side_effects=True, vmem_limit_bytes=60 * 2**20
        ),
    )(
        user_old,
        item_old,
        item_rhs,
        user_gram,
        req_count,
        flip(req_item),
        flip(req_user),
        flip(weight),
        flip(rating),
    )
    return pl.pallas_call(
        hand_on,
        out_shape=tuple(jax.ShapeDtypeStruct(array.shape, F32) for array in results),
        in_specs=[vmem] * 2,
        out_specs=(anywhere, anywhere),
        scratch_shapes=[pltpu.SemaphoreType.DMA((2,))],
        compiler_params=pltpu.CompilerParams(vmem_limit_bytes=2 * 2**20),
    )(*results)


def solution(mesh):
    in_specs = (
        P(("users", "items"), None),
        P(("users", "items"), None),
        P(("users", "items"), None),
        P(),
        P(("users", "items"), None),
        P(("users", "items"), None, None),
        P(("users", "items"), None, None),
        P(("users", "items"), None, None),
        P(("users", "items"), None, None),
    )
    out_specs = (P(("users", "items"), None), P(("users", "items"), None))
    return jax.shard_map(
        per_device, mesh=mesh, in_specs=in_specs, out_specs=out_specs, check_vma=False
    )
```
